128 devices in a mesh: box: 128 (over z, x, y, core).
Axes of the slice: x: 4, y: 4, z: 4, core: 2. Of those that a mesh axis runs over, the one named last changes fastest.
Arguments:
- self_block: bfloat16 [256, 128, 512], P('box'), may hold values from -6 to 6
- interp: bfloat16 [256, 384, 128], P('box'), may hold values from -0.5 to 0.5
- split: int32 [256, 512], P('box'), may hold values from 0 to 511, each once within a row
- inverse_block: bfloat16 [256, 384, 384], P('box'), may hold values from -0.015625 to 0.015625
- row_blocks: bfloat16 [256, 8, 128, 512], P('box'), may hold values from -6 to 6
- col_blocks: bfloat16 [256, 8, 128, 512], P('box'), may hold values from -6 to 6
- pairs: int32 [256, 24, 2], P('box'), may hold values from 0 to 7
- targets: int32 [256, 24, 2], P('box'), may hold values from 0 to 6143, as said below
- pair_blocks: bfloat16 [6144, 128, 128], P('box'), may hold values from -6 to 6
Outputs:
- updated_pairs: float32 [6144, 128, 128], P('box')
- coarse_rows: float32 [128, 4, 4, 128, 128], P('box')
The draws below stay inside these ranges and needn't reach their ends.
Inputs may be any that keep to these rules, and one draw needn't show every extreme that they name: targets[b, p, q] // 48 is an owner at most 2 devices away, along Morton order with wrap, from the device holding box b (box b lies on device b // 2); among the 96 entries of one device at most 32 name any one owner, and exactly 32 name one owner. `split`: each row is a permutation.
All inputs are finite; a program needn't handle non-finite values.
Results may differ from the reference program's by a relative error of at most 0.0047.
Values sent between devices are 32-bit elements; how exact they have to be, the bound alone decides.
No kernel may reach another device: no remote copies, remote signals or barrier semaphores. Data moves between devices by JAX's collectives and lax.ppermute only.
A program may use at most 128 MiB of HBM per device.

```python
import jax
import jax.numpy as jnp
from jax import lax

P_SIZE = 512
SK = 128
RD = 384
BOX_DEV = 2
NB = 8
PAIRS = 24
SLOTS_DEV = 48
REACH = 2
CAP = 32
BOXES_ALL = 256
SLOTS = 6144
N_BOX = 128


def draw_targets(key, part):
    key = jax.random.fold_in(key, 11)
    k_weight, k_big, k_perm, k_slot = jax.random.split(key, 4)
    count_upd = BOX_DEV * PAIRS * 2
    width_off = 2 * REACH + 1
    weights = jax.random.randint(k_weight, (N_BOX, width_off), 1, 4)
    biggest = jax.random.randint(k_big, (N_BOX,), 0, width_off)
    lanes = jnp.arange(width_off)
    is_big = lanes[None, :] == biggest[:, None]
    masked = jnp.where(is_big, 0, weights)
    remaining = count_upd - CAP
    shares = remaining * masked // jnp.sum(masked, axis=1, keepdims=True)
    leftover = remaining - jnp.sum(shares, axis=1)
    smallest = jnp.argmin(jnp.where(is_big, 10 * count_upd, shares), axis=1)
    counts = shares + jnp.where(lanes[None, :] == smallest[:, None], leftover[:, None], 0) + jnp.where(is_big, CAP, 0)
    edges = jnp.cumsum(counts, axis=1)
    ranks = jnp.arange(count_upd)
    bins = jnp.sum((ranks[None, :, None] >= edges[:, None, :]).astype(jnp.int32), axis=2)
    perm_keys = jax.random.split(k_perm, N_BOX)
    orders = jax.vmap(lambda one_key: jax.random.permutation(one_key, count_upd))(perm_keys)
    placed = jax.vmap(lambda order, binned: jnp.zeros((count_upd,), jnp.int32).at[order].set(binned.astype(jnp.int32)))(orders, bins)
    offsets = placed - REACH
    owners = (jnp.arange(N_BOX)[:, None] + offsets) % N_BOX
    slots = jax.random.randint(k_slot, (N_BOX, count_upd), 0, SLOTS_DEV)
    return (owners * SLOTS_DEV + slots).astype(jnp.int32).reshape(N_BOX * BOX_DEV, PAIRS, 2)


def set_ends(result, key, low, largest):
    place = [jax.random.randint(jax.random.fold_in(key, axis), (), 0, length) for axis, length in enumerate(result.shape)]
    main_axis = result.shape.index(max(result.shape))
    beside = place[:main_axis] + [(place[main_axis] + 1) % result.shape[main_axis]] + place[main_axis + 1:]
    return result.at[tuple(place)].set(low).at[tuple(beside)].set(largest)


def level_of(own_key, dims, cuts, low, top_value):
    loudness, own = 1.0, jax.random.fold_in(own_key, 6)
    for position, blocks in cuts:
        steps = jnp.exp(jax.random.uniform(jax.random.fold_in(own, position), (blocks,), jnp.float32, low / len(cuts), top_value / len(cuts)))
        loudness = loudness * jnp.repeat(steps, dims[position] // blocks).reshape([-1 if axis == position else 1 for axis in range(len(dims))])
    return loudness


def normal_values(stream_key, extent, deviation, most, pieces=(), kind=jnp.bfloat16):
    values = jax.random.normal(stream_key, extent, jnp.float32) * deviation
    if len(pieces) > 0:
        values = level_of(stream_key, extent, pieces, -0.22, 0.18) * values
    return jnp.clip(values, min=-most, max=most).astype(kind)


def setup_inputs(seed: int = 0) -> dict:
    key_of = jax.random.split(jax.random.key(seed), 10)
    self_block = normal_values(key_of[0], (BOXES_ALL, SK, P_SIZE), 1.0, 6.0, ((0, 128),))
    interp = normal_values(key_of[1], (BOXES_ALL, RD, SK), SK ** -0.5, 0.5, ((0, 128),))
    split = jax.vmap(lambda own: jax.random.permutation(own, P_SIZE))(jax.random.split(key_of[2], BOXES_ALL)).reshape((BOXES_ALL, P_SIZE)).astype(jnp.int32)
    inverse_block = normal_values(key_of[3], (BOXES_ALL, RD, RD), (RD * RD) ** -0.5, 0.015625, ((0, 128),))
    row_blocks = normal_values(key_of[4], (BOXES_ALL, NB, SK, P_SIZE), 1.0, 6.0, ((0, 128),))
    col_blocks = normal_values(key_of[5], (BOXES_ALL, NB, SK, P_SIZE), 1.0, 6.0, ((0, 128),))
    pairs = set_ends(jax.random.randint(key_of[6], (BOXES_ALL, PAIRS, 2), 0, NB), jax.random.fold_in(key_of[6], 1), 0, NB - 1).astype(jnp.int32)
    targets = draw_targets(jax.random.fold_in(key_of[9], 71), 0)
    pair_blocks = normal_values(key_of[8], (SLOTS, SK, SK), 1.0, 6.0, ((0, 128),))
    return {"self_block": self_block, "interp": interp, "split": split, "inverse_block": inverse_block, "row_blocks": row_blocks, "col_blocks": col_blocks, "pairs": pairs, "targets": targets, "pair_blocks": pair_blocks}


def box_terms(self_blk, interp, split, inverse, rows, cols, pairs):
    rd_count = inverse.shape[0]
    redundant = split[:rd_count]
    skeleton = split[rd_count:]
    interp_wide = interp.astype(jnp.float32)

    def compress(blocks):
        far = jnp.take(blocks, redundant, axis=2).astype(jnp.float32)
        near = jnp.take(blocks, skeleton, axis=2).astype(jnp.float32)
        return (far - jnp.einsum("nsk,rk->nsr", near, interp_wide)).astype(jnp.bfloat16)

    x_near = compress(rows)
    w_far = compress(cols)
    y_near = jnp.einsum("nsr,rq->nsq", x_near.astype(jnp.float32), inverse.astype(jnp.float32)).astype(jnp.bfloat16)
    leading = jnp.take(y_near, pairs, axis=0).astype(jnp.float32)
    trailing = jnp.take(w_far, pairs[:, ::-1], axis=0).astype(jnp.float32)
    updates = -jnp.einsum("psir,psjr->psij", leading, trailing)
    a_sr = jnp.take(self_blk, redundant, axis=1).astype(jnp.float32)
    a_ss = jnp.take(self_blk, skeleton, axis=1)
    x_self = (a_sr - jnp.dot(a_ss, interp.T, preferred_element_type=jnp.float32)).astype(jnp.bfloat16)
    y_self = jnp.dot(x_self, inverse, preferred_element_type=jnp.float32).astype(jnp.bfloat16)
    base = jnp.swapaxes(jnp.take(cols, skeleton, axis=2), 1, 2).astype(jnp.float32)
    skel_rows = base - jnp.einsum("sr,njr->nsj", y_self.astype(jnp.float32), w_far.astype(jnp.float32))
    return updates, skel_rows


def reference(self_block, interp, split, inverse_block, row_blocks, col_blocks, pairs, targets, pair_blocks):
    sk_count = pair_blocks.shape[1]

    def step(total, items):
        self_blk, interp_b, split_b, inverse_b, rows_b, cols_b, pairs_b, targets_b = items
        updates, skel_rows = box_terms(self_blk, interp_b, split_b, inverse_b, rows_b, cols_b, pairs_b)
        total = total.at[targets_b.reshape(-1)].add(updates.reshape(-1, sk_count, sk_count))
        return total, skel_rows

    start = pair_blocks.astype(jnp.float32)
    total, skel_all = lax.scan(step, start, (self_block, interp, split, inverse_block, row_blocks, col_blocks, pairs, targets))
    half = NB // 2
    shaped = skel_all.reshape(N_BOX // 2, 2, BOX_DEV, 2, half, sk_count, sk_count)
    coarse_rows = jnp.transpose(shaped, (0, 3, 1, 2, 4, 5, 6)).reshape(N_BOX, 2 * BOX_DEV, half, sk_count, sk_count)
    return total, coarse_rows
```

```python
import functools

import jax
import jax.numpy as jnp
from jax import lax
from jax.experimental import pallas as pl
from jax.experimental.pallas import tpu as pltpu
from jax.sharding import PartitionSpec as P

P_SIZE = 512
SK = 128
RD = 384
BOXES = 2
NB = 8
PAIRS = 24
SLOTS = 48
CAP = 32
ROWS = NB * SK
TILE = 256
FIRST = 32
VMEM_BYTES = 48 * 1024 * 1024
F32 = jnp.float32
BF16 = jnp.bfloat16
NT = (((1,), (1,)), ((), ()))

ANY = pl.BlockSpec(memory_space=pl.ANY)
SMEM = pl.BlockSpec(memory_space=pltpu.SMEM)
VMEM = pl.BlockSpec(memory_space=pltpu.VMEM)


def block_type(count):
    return jax.ShapeDtypeStruct((count, SK, SK), F32)


def ids_type(count):
    return jax.ShapeDtypeStruct((count,), jnp.int32)


def relation(targets, box, pair, side):
    device = lax.axis_index("box")
    devices = lax.axis_size("box")
    target = targets[box, side, pair]
    owner = lax.div(target, SLOTS)
    slot = target - owner * SLOTS
    away = owner - device
    away = jnp.where(away > devices // 2, away - devices, away)
    away = jnp.where(away < -(devices // 2), away + devices, away)
    away = jnp.where(lax.rem(device, 2) == 1, away, -away)
    return away, slot


def input_copies(hbm, vmem, sems):
    out = []
    for box in range(BOXES):
        out.append([
            pltpu.make_async_copy(source.at[box], target.at[box], sems.at[box, n])
            for n, (source, target) in enumerate(zip(hbm, vmem))
        ])
    return out


def compressor_of(split, interp, box):
    points = lax.broadcasted_iota(jnp.int32, (P_SIZE, RD), 0)
    pick_red = points == split[box:box + 1, :RD]
    points = lax.broadcasted_iota(jnp.int32, (P_SIZE, SK), 0)
    pick_skel = (points == split[box:box + 1, RD:]).astype(F32).astype(BF16)
    spread = lax.dot_general(pick_skel, interp[box], NT, preferred_element_type=F32)
    return (jnp.where(pick_red, 1.0, 0.0) - spread).astype(BF16), pick_skel


def mul(a, b):
    return jnp.dot(a, b, preferred_element_type=F32)


def products(box, copies, split, interp, inverse, rows, cols, w_far, compressor, grams):
    copies[0].wait()
    comp, pick_skel = compressor_of(split, interp, box)
    compressor[...] = comp
    copies[1].wait()

    def far(n, _):
        at = pl.ds(pl.multiple_of(n * TILE, TILE), TILE)
        w_far[at, :] = mul(cols[box, at, :], compressor[...]).astype(BF16)
        return 0

    lax.fori_loop(0, ROWS // TILE, far, 0)
    copies[2].wait()
    copies[3].wait()

    def near(n, _):
        at = pl.ds(pl.multiple_of(n * TILE, TILE), TILE)
        x_near = mul(rows[box, at, :], compressor[...]).astype(BF16)
        y_near = mul(x_near, inverse[box]).astype(BF16)
        tile = lax.dot_general(y_near, w_far[...], NT, preferred_element_type=F32)
        for k in range(TILE // SK):
            for j in range(NB):
                grams[n * (TILE // SK) + k, j] = tile[k * SK:(k + 1) * SK, j * SK:(j + 1) * SK]
        return 0

    lax.fori_loop(0, ROWS // TILE, near, 0)
    return pick_skel


def front_kernel(targets, pairs, split, interp_h, cols_h, rows_h, inverse_h, near_out, near_ids, far_out, far_ids,
                 interp, cols, rows, inverse, w_far, compressor, grams, acc, used, in_sems, out_sems):
    copies = input_copies((interp_h, cols_h, rows_h, inverse_h), (interp, cols, rows, inverse), in_sems)
    for box in range(BOXES):
        for copy in copies[box]:
            copy.start()

    def clear(n, _):
        acc[n] = jnp.zeros((SK, SK), F32)
        used[n] = 0
        return 0

    lax.fori_loop(0, 2 * SLOTS, clear, 0)

    def clear_ids(n, _):
        near_ids[n] = -1
        far_ids[n] = -1
        return 0

    lax.fori_loop(0, CAP, clear_ids, 0)

    for box in range(BOXES):
        products(box, copies[box], split, interp, inverse, rows, cols, w_far, compressor, grams)

        def add(n, _):
            pair = lax.div(n, 2)
            side = lax.rem(n, 2)
            away, slot = relation(targets, box, pair, side)

            @pl.when((away == 2) | (away == -2))
            def _():
                place = jnp.where(away == 2, slot, slot + SLOTS)
                used[place] = 1
                acc[place] = acc[place] - grams[pairs[box, side, pair], pairs[box, 1 - side, pair]]

            return 0

        lax.fori_loop(0, 2 * PAIRS, add, 0)

    for base, out, ids in ((0, near_out, near_ids), (SLOTS, far_out, far_ids)):

        def send(n, count):
            @pl.when(used[base + n] == 1)
            def _():
                ids[count] = n
                pltpu.make_async_copy(acc.at[base + n], out.at[count], out_sems.at[base + n]).start()

            return count + used[base + n]

        lax.fori_loop(0, SLOTS, send, 0)

    for base, out in ((0, near_out), (SLOTS, far_out)):

        def drain(n, _):
            @pl.when(used[base + n] == 1)
            def _():
                pltpu.make_async_copy(acc.at[base + n], out.at[0], out_sems.at[base + n]).wait()

            return 0

        lax.fori_loop(0, SLOTS, drain, 0)


def box_scratch():
    return [
        pltpu.VMEM((BOXES, RD, SK), BF16),
        pltpu.VMEM((BOXES, ROWS, P_SIZE), BF16),
        pltpu.VMEM((BOXES, ROWS, P_SIZE), BF16),
        pltpu.VMEM((BOXES, RD, RD), BF16),
        pltpu.VMEM((ROWS, RD), BF16),
        pltpu.VMEM((P_SIZE, RD), BF16),
        pltpu.VMEM((NB, NB, SK, SK), F32),
    ]


def front(targets, pairs, split, interp, cols, rows, inverse):
    return pl.pallas_call(
        front_kernel,
        out_shape=(block_type(CAP), ids_type(CAP), block_type(CAP), ids_type(CAP)),
        in_specs=[SMEM, SMEM, VMEM, ANY, ANY, ANY, ANY],
        out_specs=(ANY, SMEM, ANY, SMEM),
        scratch_shapes=box_scratch() + [
            pltpu.VMEM((2 * SLOTS, SK, SK), F32),
            pltpu.SMEM((2 * SLOTS,), jnp.int32),
            pltpu.SemaphoreType.DMA((BOXES, 4)),
            pltpu.SemaphoreType.DMA((2 * SLOTS,)),
        ],
        compiler_params=pltpu.CompilerParams(vmem_limit_bytes=VMEM_BYTES),
        cost_estimate=pl.CostEstimate(flops=4_000_000_000, bytes_accessed=10_000_000, transcendentals=0),
        name="front",
    )(targets, pairs, split, interp, cols, rows, inverse)


def rest_kernel(targets, pairs, split, interp_h, cols_h, rows_h, inverse_h, self_h, start_h,
                edge_out, partner_out, total_out, coarse_out, skel_out,
                interp, cols, rows, inverse, self_block, w_far, compressor, grams, start, acc, skel, in_sems, out_sems):
    copies = input_copies((interp_h, cols_h, rows_h, inverse_h, self_h), (interp, cols, rows, inverse, self_block), in_sems)
    start_copy = pltpu.make_async_copy(start_h, start, out_sems.at[5])
    for copy in copies[0]:
        copy.start()
    start_copy.start()
    for copy in copies[1]:
        copy.start()

    def clear(n, _):
        acc[n] = jnp.zeros((SK, SK), F32)
        return 0

    lax.fori_loop(0, 2 * SLOTS, clear, 0)
    start_copy.wait()

    def widen(n, _):
        acc[2 * SLOTS + n] = start[n].astype(F32)
        return 0

    lax.fori_loop(0, SLOTS, widen, 0)
    parity = lax.rem(lax.axis_index("box"), 2)

    for box in range(BOXES):
        pick_skel = products(box, copies[box], split, interp, inverse, rows, cols, w_far, compressor, grams)

        def add(n, _):
            pair = lax.div(n, 2)
            side = lax.rem(n, 2)
            away, slot = relation(targets, box, pair, side)

            @pl.when((away <= 1) & (away >= -1))
            def _():
                place = slot + jnp.where(away == 0, 2 * SLOTS, jnp.where(away == 1, 0, SLOTS))
                acc[place] = acc[place] - grams[pairs[box, side, pair], pairs[box, 1 - side, pair]]

            return 0

        lax.fori_loop(0, 2 * PAIRS, add, 0)
        copies[box][4].wait()
        x_self = mul(self_block[box], compressor[...]).astype(BF16)
        y_self = mul(x_self, inverse[box]).astype(BF16)
        pick_rows = pick_skel.astype(F32).T.astype(BF16)
        for n in range(ROWS // TILE):
            at = slice(n * TILE, (n + 1) * TILE)
            base = lax.dot_general(pick_rows, cols[box, at, :], NT, preferred_element_type=F32)
            base = base - lax.dot_general(y_self, w_far[at, :], NT, preferred_element_type=F32)
            for k in range(TILE // SK):
                j = n * (TILE // SK) + k
                skel[j // 4, box, j % 4] = base[:, k * SK:(k + 1) * SK]

    outs = [
        pltpu.make_async_copy(acc.at[pl.ds(0, SLOTS)], edge_out, out_sems.at[0]),
        pltpu.make_async_copy(acc.at[pl.ds(SLOTS, SLOTS)], partner_out, out_sems.at[1]),
        pltpu.make_async_copy(acc.at[pl.ds(2 * SLOTS, SLOTS)], total_out, out_sems.at[2]),
        pltpu.make_async_copy(skel.at[parity], coarse_out.at[pl.ds(2 * parity, 2)], out_sems.at[3]),
        pltpu.make_async_copy(skel.at[1 - parity], skel_out, out_sems.at[4]),
    ]
    for copy in outs:
        copy.start()
    for copy in outs:
        copy.wait()


def rest(targets, pairs, split, interp, cols, rows, inverse, self_block, start):
    scratch = box_scratch()
    scratch.insert(4, pltpu.VMEM((BOXES, SK, P_SIZE), BF16))
    return pl.pallas_call(
        rest_kernel,
        out_shape=(
            block_type(SLOTS), block_type(SLOTS), block_type(SLOTS),
            jax.ShapeDtypeStruct((2 * BOXES, NB // 2, SK, SK), F32),
            jax.ShapeDtypeStruct((BOXES, NB // 2, SK, SK), F32),
        ),
        in_specs=[SMEM, SMEM, VMEM] + [ANY] * 6,
        out_specs=(ANY,) * 5,
        scratch_shapes=scratch + [
            pltpu.VMEM((SLOTS, SK, SK), BF16),
            pltpu.VMEM((3 * SLOTS, SK, SK), F32),
            pltpu.VMEM((2, BOXES, NB // 2, SK, SK), F32),
            pltpu.SemaphoreType.DMA((BOXES, 5)),
            pltpu.SemaphoreType.DMA((6,)),
        ],
        compiler_params=pltpu.CompilerParams(vmem_limit_bytes=VMEM_BYTES),
        cost_estimate=pl.CostEstimate(flops=4_400_000_000, bytes_accessed=20_000_000, transcendentals=0),
        name="rest",
    )(targets, pairs, split, interp, cols, rows, inverse, self_block, start)


def merge_kernel(ids, edge, arrived, first, second):
    first[...] = edge[:FIRST]
    second[...] = edge[FIRST:]

    def add(n, _):
        slot = ids[n]

        @pl.when((slot >= 0) & (slot < FIRST))
        def _():
            first[slot] = first[slot] + arrived[n]

        @pl.when(slot >= FIRST)
        def _():
            second[slot - FIRST] = second[slot - FIRST] + arrived[n]

        return 0

    lax.fori_loop(0, CAP, add, 0)


def merge(ids, edge, arrived):
    return pl.pallas_call(
        merge_kernel,
        out_shape=(block_type(FIRST), block_type(SLOTS - FIRST)),
        in_specs=[SMEM, VMEM, VMEM],
        out_specs=(VMEM, VMEM),
        compiler_params=pltpu.CompilerParams(vmem_limit_bytes=VMEM_BYTES),
        cost_estimate=pl.CostEstimate(flops=1_000_000, bytes_accessed=9_000_000, transcendentals=0),
        name="merge",
    )(ids, edge, arrived)


def add_compact_kernel(ids, total, partner, arrived, out):
    out[...] = total[...] + partner[...]

    def add(n, _):
        slot = ids[n]

        @pl.when(slot >= 0)
        def _():
            out[slot] = out[slot] + arrived[n]

        return 0

    lax.fori_loop(0, CAP, add, 0)


def add_compact(ids, total, partner, arrived):
    return pl.pallas_call(
        add_compact_kernel,
        out_shape=block_type(SLOTS),
        in_specs=[SMEM, VMEM, VMEM, VMEM],
        out_specs=VMEM,
        compiler_params=pltpu.CompilerParams(vmem_limit_bytes=VMEM_BYTES),
        cost_estimate=pl.CostEstimate(flops=2_000_000, bytes_accessed=12_000_000, transcendentals=0),
        name="add_compact",
    )(ids, total, partner, arrived)


def add_dense_kernel(total, arrived, out):
    out[...] = total[...] + arrived[...]


def add_dense(total, arrived, begin, step):
    count = arrived.shape[0]
    here = pl.BlockSpec((step, SK, SK), lambda n: (n + begin // step, 0, 0))
    return pl.pallas_call(
        add_dense_kernel,
        out_shape=block_type(SLOTS),
        grid=(count // step,),
        in_specs=[here, pl.BlockSpec((step, SK, SK), lambda n: (n, 0, 0))],
        out_specs=here,
        input_output_aliases={0: 0},
        cost_estimate=pl.CostEstimate(flops=1_000_000, bytes_accessed=count * 3 * 65536, transcendentals=0),
        name="add_dense",
    )(total, arrived)


def place_kernel(coarse, received, out, sem):
    parity = lax.rem(lax.axis_index("box"), 2)
    copy = pltpu.make_async_copy(received, out.at[pl.ds(2 - 2 * parity, 2)], sem)
    copy.start()
    copy.wait()


def place(coarse, received):
    return pl.pallas_call(
        place_kernel,
        out_shape=jax.ShapeDtypeStruct(coarse.shape, F32),
        in_specs=[ANY, ANY],
        out_specs=ANY,
        scratch_shapes=[pltpu.SemaphoreType.DMA],
        input_output_aliases={0: 0},
        cost_estimate=pl.CostEstimate(flops=0, bytes_accessed=1_000_000, transcendentals=0),
        name="place",
    )(coarse, received)


def moved(value, route):
    devices = lax.axis_size("box")
    return lax.ppermute(value, "box", [(i, route(i) % devices) for i in range(devices)])


def other_core(i):
    return i ^ 1


def across(i):
    return i + 1 if i % 2 else i - 1


def beyond(i):
    return i + 2 if i % 2 else i - 2


def body(self_block, interp, split, inverse_block, row_blocks, col_blocks, pairs, targets, pair_blocks):
    targets = jnp.transpose(targets, (0, 2, 1))
    pairs = jnp.transpose(pairs, (0, 2, 1))
    rows = row_blocks.reshape(BOXES, ROWS, P_SIZE)
    cols = col_blocks.reshape(BOXES, ROWS, P_SIZE)
    near, near_ids, far, far_ids = front(targets, pairs, split, interp, cols, rows, inverse_block)
    near, near_ids = moved((near, near_ids), beyond)
    far, far_ids = moved((far, far_ids), other_core)
    edge, partner, total, coarse, skel = rest(
        targets, pairs, split, interp, cols, rows, inverse_block, self_block, pair_blocks
    )
    first, second = merge(far_ids, edge, far)
    first = moved(first, across)
    second = moved(second, across)
    partner = moved(partner, other_core)
    skel = moved(skel, other_core)
    coarse = place(coarse, skel)
    total = add_compact(near_ids, total, partner, near)
    total = add_dense(total, first, 0, 8)
    total = add_dense(total, second, FIRST, 4)
    return total, coarse[None]


def solution(mesh):
    return jax.shard_map(
        body,
        mesh=mesh,
        in_specs=(
            P("box", None, None),
            P("box", None, None),
            P("box", None),
            P("box", None, None),
            P("box", None, None, None),
            P("box", None, None, None),
            P("box", None, None),
            P("box", None, None),
            P("box", None, None),
        ),
        out_specs=(P("box", None, None), P("box", None, None, None, None)),
        check_vma=False,
    )
```

```python
import functools

import jax
import jax.numpy as jnp
from jax import lax
from jax.experimental import pallas as pl
from jax.experimental.pallas import tpu as pltpu
from jax.sharding import PartitionSpec as P

P_SIZE = 512
SK = 128
RD = 384
BOXES = 2
NB = 8
PAIRS = 24
SLOTS = 48
CAP = 32
ROWS = NB * SK
TILE = 512
FIRST = 32
VMEM_BYTES = 62 * 1024 * 1024
F32 = jnp.float32
BF16 = jnp.bfloat16
NT = (((1,), (1,)), ((), ()))

ANY = pl.BlockSpec(memory_space=pl.ANY)
VMEM = pl.BlockSpec(memory_space=pltpu.VMEM)


def block_type(count):
    return jax.ShapeDtypeStruct((count, SK, SK), F32)


def cost(us):
    return pl.CostEstimate(flops=us * 1_000_000_000, bytes_accessed=0, transcendentals=0)


def payload_type(count):
    return jax.ShapeDtypeStruct((count * SK + 8, SK), F32)


def input_copies(hbm, vmem, sems):
    out = []
    for box in range(BOXES):
        out.append([
            pltpu.make_async_copy(source.at[box], target.at[box], sems.at[box, n])
            for n, (source, target) in enumerate(zip(hbm, vmem))
        ])
    return out


def compressor_of(split, interp, box):
    points = lax.broadcasted_iota(jnp.int32, (P_SIZE, RD), 0)
    pick_red = points == split[box:box + 1, :RD]
    points = lax.broadcasted_iota(jnp.int32, (P_SIZE, SK), 0)
    pick_skel = (points == split[box:box + 1, RD:]).astype(F32).astype(BF16)
    spread = lax.dot_general(pick_skel, interp[box], NT, preferred_element_type=F32)
    return (jnp.where(pick_red, 1.0, 0.0) - spread).astype(BF16), pick_skel


def mul(a, b):
    return jnp.dot(a, b, preferred_element_type=F32)


def products(box, copies, split, interp, inverse, rows, cols, w_far, y_near, compressor, grams):
    copies[0].wait()
    comp, pick_skel = compressor_of(split, interp, box)
    compressor[...] = comp
    copies[1].wait()

    def far(n, _):
        at = pl.ds(pl.multiple_of(n * TILE, TILE), TILE)
        w_far[at, :] = mul(cols[box, at, :], compressor[...]).astype(BF16)
        return 0

    lax.fori_loop(0, ROWS // TILE, far, 0, unroll=True)
    copies[2].wait()
    copies[3].wait()

    def near(n, _):
        at = pl.ds(pl.multiple_of(n * TILE, TILE), TILE)
        x_near = mul(rows[box, at, :], compressor[...]).astype(BF16)
        y_near[at, :] = mul(x_near, inverse[box]).astype(BF16)
        return 0

    lax.fori_loop(0, ROWS // TILE, near, 0, unroll=True)

    def gram(n, _):
        at = pl.ds(pl.multiple_of(n * TILE, TILE), TILE)
        tile = lax.dot_general(y_near[...], w_far[at, :], NT, preferred_element_type=F32)
        for i in range(NB):
            for k in range(TILE // SK):
                grams[i, n * (TILE // SK) + k] = tile[i * SK:(i + 1) * SK, k * SK:(k + 1) * SK]
        return 0

    lax.fori_loop(0, ROWS // TILE, gram, 0, unroll=True)
    return pick_skel


def front_kernel(targets_h, pairs_h, split, interp_h, cols_h, rows_h, inverse_h, near_out, far_out,
                 interp, cols, rows, inverse, w_far, y_near, compressor, grams, acc, targets, pairs, used, todo, near_ids, far_ids, in_sems, out_sems, small_sems):
    small = [
        pltpu.make_async_copy(targets_h, targets, small_sems.at[0]),
        pltpu.make_async_copy(pairs_h, pairs, small_sems.at[1]),
    ]
    for copy in small:
        copy.start()
    copies = input_copies((interp_h, cols_h, rows_h, inverse_h), (interp, cols, rows, inverse), in_sems)
    for box in range(BOXES):
        for copy in copies[box]:
            copy.start()

    def clear_used(n, _):
        used[n] = 0
        return 0

    lax.fori_loop(0, 2 * SLOTS, clear_used, 0, unroll=8)
    device = lax.axis_index("box")
    odd = lax.rem(device, 2)
    all_slots = lax.axis_size("box") * SLOTS
    here = device * SLOTS
    for copy in small:
        copy.wait()

    ends = []
    for box in range(BOXES):

        def enter(pair, end):
            numbers = [pairs[box, 0, pair], pairs[box, 1, pair]]
            for side in range(2):
                away = targets[box, side, pair] - here
                away = jnp.where(away >= all_slots // 2, away - all_slots, away)
                away = jnp.where(away < -(all_slots // 2), away + all_slots, away)
                ahead = away >= 2 * SLOTS
                wanted = ahead | (away < -SLOTS)
                slot = jnp.where(ahead, away - 2 * SLOTS, away + 2 * SLOTS)
                near = ahead.astype(jnp.int32) == odd
                place = jnp.where(wanted, jnp.where(near, slot, slot + SLOTS), 2 * SLOTS)
                todo[box, end] = place * 128 + numbers[side] * 16 + numbers[1 - side] * 2 + used[place]
                used[place] = 1
                end = end + wanted.astype(jnp.int32)
            return end

        ends.append(lax.fori_loop(0, PAIRS, enter, jnp.int32(0), unroll=2))

    def number(n, counts):
        out = []
        for base, ids, count in ((0, near_ids, counts[0]), (SLOTS, far_ids, counts[1])):
            ids[0, count] = n.astype(F32)
            out.append(count + used[base + n])
        return tuple(out)

    counts = lax.fori_loop(0, SLOTS, number, (jnp.int32(0), jnp.int32(0)), unroll=4)
    for ids, count in ((near_ids, counts[0]), (far_ids, counts[1])):

        def blank(n, _):
            ids[0, n] = -1.0
            return 0

        lax.fori_loop(count, CAP, blank, 0)

    for box in range(BOXES):
        products(box, copies[box], split, interp, inverse, rows, cols, w_far, y_near, compressor, grams)

        def add(n, _):
            entry = todo[box, n]
            place = lax.shift_right_logical(entry, 7)
            i = lax.shift_right_logical(entry, 4) & 7
            j = lax.shift_right_logical(entry, 1) & 7
            before = acc[place]
            acc[place] = jnp.where((entry & 1) == 1, before, 0.0) - grams[i, j]
            return 0

        lax.fori_loop(0, ends[box], add, 0)

    labels = [
        pltpu.make_async_copy(near_ids, near_out.at[pl.ds(CAP * SK, 8)], small_sems.at[0]),
        pltpu.make_async_copy(far_ids, far_out.at[pl.ds(CAP * SK, 8)], small_sems.at[1]),
    ]
    for copy in labels:
        copy.start()
    for base, out, ids, count in ((0, near_out, near_ids, counts[0]), (SLOTS, far_out, far_ids, counts[1])):

        def send(n, _):
            pltpu.make_async_copy(acc.at[base + ids[0, n].astype(jnp.int32)], out.at[pl.ds(pl.multiple_of(n * SK, SK), SK)], out_sems.at[base + n]).start()
            return 0

        lax.fori_loop(0, count, send, 0)

    for base, out, ids, count in ((0, near_out, near_ids, counts[0]), (SLOTS, far_out, far_ids, counts[1])):

        def drain(n, _):
            pltpu.make_async_copy(acc.at[base], out.at[pl.ds(0, SK)], out_sems.at[base + n]).wait()
            return 0

        lax.fori_loop(0, count, drain, 0)

    for copy in labels:
        copy.wait()


def box_scratch():
    return [
        pltpu.VMEM((BOXES, RD, SK), BF16),
        pltpu.VMEM((BOXES, ROWS, P_SIZE), BF16),
        pltpu.VMEM((BOXES, ROWS, P_SIZE), BF16),
        pltpu.VMEM((BOXES, RD, RD), BF16),
        pltpu.VMEM((ROWS, RD), BF16),
        pltpu.VMEM((ROWS, RD), BF16),
        pltpu.VMEM((P_SIZE, RD), BF16),
        pltpu.VMEM((NB, NB, SK, SK), F32),
    ]


def front(targets, pairs, split, interp, cols, rows, inverse):
    return pl.pallas_call(
        front_kernel,
        out_shape=(payload_type(CAP), payload_type(CAP)),
        in_specs=[ANY, ANY, VMEM, ANY, ANY, ANY, ANY],
        out_specs=(ANY, ANY),
        scratch_shapes=box_scratch() + [
            pltpu.VMEM((2 * SLOTS, SK, SK), F32),
            pltpu.SMEM((BOXES, 2, PAIRS), jnp.int32),
            pltpu.SMEM((BOXES, 2, PAIRS), jnp.int32),
            pltpu.SMEM((2 * SLOTS + 1,), jnp.int32),
            pltpu.SMEM((BOXES, 2 * PAIRS + 1), jnp.int32),
            pltpu.SMEM((8, 128), F32),
            pltpu.SMEM((8, 128), F32),
            pltpu.SemaphoreType.DMA((BOXES, 4)),
            pltpu.SemaphoreType.DMA((2 * SLOTS,)),
            pltpu.SemaphoreType.DMA((2,)),
        ],
        compiler_params=pltpu.CompilerParams(vmem_limit_bytes=VMEM_BYTES),
        cost_estimate=cost(1),
        name="front",
    )(targets, pairs, split, interp, cols, rows, inverse)


def rest_kernel(targets_h, pairs_h, split, interp_h, cols_h, rows_h, inverse_h, start_h,
                edge_out, partner_out, total_out,
                interp, cols, rows, inverse, w_far, y_near, compressor, grams, start, acc, targets, pairs, todo,
                in_sems, out_sems, small_sems):
    small = [
        pltpu.make_async_copy(targets_h, targets, small_sems.at[0]),
        pltpu.make_async_copy(pairs_h, pairs, small_sems.at[1]),
    ]
    for copy in small:
        copy.start()
    copies = input_copies((interp_h, cols_h, rows_h, inverse_h), (interp, cols, rows, inverse), in_sems)
    start_copy = pltpu.make_async_copy(start_h, start, out_sems.at[3])
    for copy in copies[0]:
        copy.start()
    start_copy.start()
    for copy in copies[1]:
        copy.start()

    def clear(n, _):
        acc[n] = jnp.zeros((SK, SK), F32)
        return 0

    lax.fori_loop(0, 2 * SLOTS, clear, 0)
    device = lax.axis_index("box")
    odd = lax.rem(device, 2)
    all_slots = lax.axis_size("box") * SLOTS
    here = device * SLOTS
    for copy in small:
        copy.wait()

    def enter(pair, ends):
        out = []
        for box in range(BOXES):
            end = ends[box]
            numbers = [pairs[box, 0, pair], pairs[box, 1, pair]]
            for side in range(2):
                away = targets[box, side, pair] - here
                away = jnp.where(away >= all_slots // 2, away - all_slots, away)
                away = jnp.where(away < -(all_slots // 2), away + all_slots, away)
                ahead = away >= SLOTS
                behind = away < 0
                wanted = (away < 2 * SLOTS) & (away >= -SLOTS)
                edge = ahead.astype(jnp.int32) == odd
                place = jnp.where(
                    ahead | behind,
                    jnp.where(ahead, away - SLOTS, away + SLOTS) + jnp.where(edge, 0, SLOTS),
                    away + 2 * SLOTS,
                )
                todo[box, end] = place * 64 + numbers[side] * 8 + numbers[1 - side]
                end = end + wanted.astype(jnp.int32)
            out.append(end)
        return tuple(out)

    ends = lax.fori_loop(0, PAIRS, enter, (jnp.int32(0), jnp.int32(0)))
    start_copy.wait()

    def widen(n, _):
        acc[2 * SLOTS + n] = start[n].astype(F32)
        return 0

    lax.fori_loop(0, SLOTS, widen, 0)
    for box in range(BOXES):
        products(box, copies[box], split, interp, inverse, rows, cols, w_far, y_near, compressor, grams)

        def add(n, _):
            entry = todo[box, n]
            place = lax.shift_right_logical(entry, 6)
            i = lax.shift_right_logical(entry, 3) & 7
            j = entry & 7
            acc[place] = acc[place] - grams[i, j]
            return 0

        lax.fori_loop(0, ends[box], add, 0)

    outs = [
        pltpu.make_async_copy(acc.at[pl.ds(0, SLOTS)], edge_out, out_sems.at[0]),
        pltpu.make_async_copy(acc.at[pl.ds(SLOTS, SLOTS)], partner_out, out_sems.at[1]),
        pltpu.make_async_copy(acc.at[pl.ds(2 * SLOTS, SLOTS)], total_out, out_sems.at[2]),
    ]
    for copy in outs:
        copy.start()
    for copy in outs:
        copy.wait()


def rest(targets, pairs, split, interp, cols, rows, inverse, start):
    return pl.pallas_call(
        rest_kernel,
        out_shape=(block_type(SLOTS), block_type(SLOTS), block_type(SLOTS)),
        in_specs=[ANY, ANY, VMEM] + [ANY] * 5,
        out_specs=(ANY,) * 3,
        scratch_shapes=box_scratch() + [
            pltpu.VMEM((SLOTS, SK, SK), BF16),
            pltpu.VMEM((3 * SLOTS, SK, SK), F32),
            pltpu.SMEM((BOXES, 2, PAIRS), jnp.int32),
            pltpu.SMEM((BOXES, 2, PAIRS), jnp.int32),
            pltpu.SMEM((BOXES, 2 * PAIRS + 1), jnp.int32),
            pltpu.SemaphoreType.DMA((BOXES, 4)),
            pltpu.SemaphoreType.DMA((4,)),
            pltpu.SemaphoreType.DMA((2,)),
        ],
        compiler_params=pltpu.CompilerParams(vmem_limit_bytes=VMEM_BYTES),
        cost_estimate=cost(1),
        name="rest",
    )(targets, pairs, split, interp, cols, rows, inverse, start)


def skeletons_kernel(after, split, interp_h, cols_h, inverse_h, self_h, coarse_out, skel_out,
                     interp, cols, inverse, self_block, w_far, skel, in_sems, out_sems):
    copies = input_copies((interp_h, cols_h, inverse_h, self_h), (interp, cols, inverse, self_block), in_sems)
    for box in range(BOXES):
        for copy in copies[box]:
            copy.start()
    parity = lax.rem(lax.axis_index("box"), 2)
    for box in range(BOXES):
        for copy in copies[box]:
            copy.wait()
        comp, pick_skel = compressor_of(split, interp, box)
        x_self = mul(self_block[box], comp).astype(BF16)
        y_self = mul(x_self, inverse[box]).astype(BF16)
        pick_rows = pick_skel.astype(F32).T.astype(BF16)
        w_far[...] = mul(cols[box], comp).astype(BF16)
        for n in range(ROWS // TILE):
            at = slice(n * TILE, (n + 1) * TILE)
            base = lax.dot_general(pick_rows, cols[box, at, :], NT, preferred_element_type=F32)
            base = base - lax.dot_general(y_self, w_far[at, :], NT, preferred_element_type=F32)
            for k in range(TILE // SK):
                j = n * (TILE // SK) + k
                skel[j // 4, box, j % 4] = base[:, k * SK:(k + 1) * SK]
    outs = [
        pltpu.make_async_copy(skel.at[parity], coarse_out.at[pl.ds(2 * parity, 2)], out_sems.at[0]),
        pltpu.make_async_copy(skel.at[1 - parity], skel_out, out_sems.at[1]),
    ]
    for copy in outs:
        copy.start()
    for copy in outs:
        copy.wait()


def skeletons(after, split, interp, cols, inverse, self_block):
    return pl.pallas_call(
        skeletons_kernel,
        out_shape=(
            jax.ShapeDtypeStruct((2 * BOXES, NB // 2, SK, SK), F32),
            jax.ShapeDtypeStruct((BOXES, NB // 2, SK, SK), F32),
        ),
        in_specs=[ANY, VMEM] + [ANY] * 4,
        out_specs=(ANY,) * 2,
        scratch_shapes=[
            pltpu.VMEM((BOXES, RD, SK), BF16),
            pltpu.VMEM((BOXES, ROWS, P_SIZE), BF16),
            pltpu.VMEM((BOXES, RD, RD), BF16),
            pltpu.VMEM((BOXES, SK, P_SIZE), BF16),
            pltpu.VMEM((ROWS, RD), BF16),
            pltpu.VMEM((2, BOXES, NB // 2, SK, SK), F32),
            pltpu.SemaphoreType.DMA((BOXES, 4)),
            pltpu.SemaphoreType.DMA((2,)),
        ],
        compiler_params=pltpu.CompilerParams(vmem_limit_bytes=VMEM_BYTES),
        cost_estimate=cost(1),
        name="skeletons",
    )(after, split, interp, cols, inverse, self_block)


def compact(payload, blocks, ids, sems):
    height = blocks.shape[0]
    return [
        pltpu.make_async_copy(payload.at[pl.ds(height, 8)], ids, sems.at[0]),
        pltpu.make_async_copy(payload.at[pl.ds(0, height)], blocks, sems.at[1]),
    ]


def merge_kernel(edge_h, payload, first_out, second_out, edge, blocks, ids, sems):
    copies = compact(payload, blocks, ids, sems) + [pltpu.make_async_copy(edge_h, edge, sems.at[2])]
    for copy in copies:
        copy.start()
    for copy in copies:
        copy.wait()

    def add(n, _):
        slot = ids[0, n].astype(jnp.int32)

        @pl.when(slot >= 0)
        def _():
            edge[slot] = edge[slot] + blocks[pl.ds(pl.multiple_of(n * SK, SK), SK), :]

        return 0

    lax.fori_loop(0, CAP, add, 0)
    outs = [
        pltpu.make_async_copy(edge.at[pl.ds(0, FIRST)], first_out, sems.at[0]),
        pltpu.make_async_copy(edge.at[pl.ds(FIRST, SLOTS - FIRST)], second_out, sems.at[1]),
    ]
    for copy in outs:
        copy.start()
    for copy in outs:
        copy.wait()


def merge(edge, payload):
    return pl.pallas_call(
        merge_kernel,
        out_shape=(block_type(FIRST), block_type(SLOTS - FIRST)),
        in_specs=[ANY, ANY],
        out_specs=(ANY, ANY),
        scratch_shapes=[
            pltpu.VMEM((SLOTS, SK, SK), F32),
            pltpu.VMEM((CAP * SK, SK), F32),
            pltpu.SMEM((8, 128), F32),
            pltpu.SemaphoreType.DMA((3,)),
        ],
        compiler_params=pltpu.CompilerParams(vmem_limit_bytes=VMEM_BYTES),
        cost_estimate=cost(1),
        name="merge",
    )(edge, payload)


def add_compact_kernel(total_h, payload, out, total, blocks, ids, sems):
    copies = compact(payload, blocks, ids, sems) + [pltpu.make_async_copy(total_h, total, sems.at[2])]
    for copy in copies:
        copy.start()
    for copy in copies:
        copy.wait()

    def add(n, _):
        slot = ids[0, n].astype(jnp.int32)

        @pl.when(slot >= 0)
        def _():
            total[slot] = total[slot] + blocks[pl.ds(pl.multiple_of(n * SK, SK), SK), :]

        return 0

    lax.fori_loop(0, CAP, add, 0)
    copy = pltpu.make_async_copy(total, out, sems.at[0])
    copy.start()
    copy.wait()


def add_compact(total, payload):
    return pl.pallas_call(
        add_compact_kernel,
        out_shape=block_type(SLOTS),
        in_specs=[ANY, ANY],
        out_specs=ANY,
        scratch_shapes=[
            pltpu.VMEM((SLOTS, SK, SK), F32),
            pltpu.VMEM((CAP * SK, SK), F32),
            pltpu.SMEM((8, 128), F32),
            pltpu.SemaphoreType.DMA((3,)),
        ],
        input_output_aliases={0: 0},
        compiler_params=pltpu.CompilerParams(vmem_limit_bytes=VMEM_BYTES),
        cost_estimate=cost(1000),
        name="add_compact",
    )(total, payload)


def add_dense_kernel(step, begin, total_h, arrived, out, total, blocks, sems):
    count = arrived.shape[0] // step
    loads = []
    for n in range(count):
        loads.append((
            pltpu.make_async_copy(total_h.at[pl.ds(begin + n * step, step)], total.at[n], sems.at[n, 0]),
            pltpu.make_async_copy(arrived.at[pl.ds(n * step, step)], blocks.at[n], sems.at[n, 1]),
        ))
    for pair in loads:
        for copy in pair:
            copy.start()
    stores = []
    for n in range(count):
        for copy in loads[n]:
            copy.wait()
        total[n] = total[n] + blocks[n]
        stores.append(pltpu.make_async_copy(total.at[n], out.at[pl.ds(begin + n * step, step)], sems.at[n, 2]))
        stores[n].start()
    for copy in stores:
        copy.wait()


def add_dense(total, arrived, begin, step):
    count = arrived.shape[0] // step
    return pl.pallas_call(
        functools.partial(add_dense_kernel, step, begin),
        out_shape=block_type(SLOTS),
        in_specs=[ANY, ANY],
        out_specs=ANY,
        scratch_shapes=[
            pltpu.VMEM((count, step, SK, SK), F32),
            pltpu.VMEM((count, step, SK, SK), F32),
            pltpu.SemaphoreType.DMA((count, 3)),
        ],
        input_output_aliases={0: 0},
        compiler_params=pltpu.CompilerParams(vmem_limit_bytes=VMEM_BYTES),
        cost_estimate=cost(1),
        name="add_dense",
    )(total, arrived)


def place_kernel(coarse, received, out, held, sems):
    parity = lax.rem(lax.axis_index("box"), 2)
    copy = pltpu.make_async_copy(received, held, sems.at[0])
    copy.start()
    copy.wait()
    copy = pltpu.make_async_copy(held, out.at[pl.ds(2 - 2 * parity, 2)], sems.at[1])
    copy.start()
    copy.wait()


def place(coarse, received):
    return pl.pallas_call(
        place_kernel,
        out_shape=jax.ShapeDtypeStruct(coarse.shape, F32),
        in_specs=[ANY, ANY],
        out_specs=ANY,
        scratch_shapes=[pltpu.VMEM((BOXES, NB // 2, SK, SK), F32), pltpu.SemaphoreType.DMA((2,))],
        input_output_aliases={0: 0},
        compiler_params=pltpu.CompilerParams(vmem_limit_bytes=VMEM_BYTES),
        cost_estimate=cost(1),
        name="place",
    )(coarse, received)


def moved(value, route):
    devices = lax.axis_size("box")
    return lax.ppermute(value, "box", [(i, route(i) % devices) for i in range(devices)])


def other_core(i):
    return i ^ 1


def across(i):
    return i + 1 if i % 2 else i - 1


def beyond(i):
    return i + 2 if i % 2 else i - 2


def body(self_block, interp, split, inverse_block, row_blocks, col_blocks, pairs, targets, pair_blocks):
    targets = jnp.transpose(targets, (0, 2, 1))
    pairs = jnp.transpose(pairs, (0, 2, 1))
    rows = row_blocks.reshape(BOXES, ROWS, P_SIZE)
    cols = col_blocks.reshape(BOXES, ROWS, P_SIZE)
    near, far = front(targets, pairs, split, interp, cols, rows, inverse_block)
    near = moved(near, beyond)
    far = moved(far, other_core)
    edge, partner, total = rest(targets, pairs, split, interp, cols, rows, inverse_block, pair_blocks)
    first, second = merge(edge, far)
    first = moved(first, across)
    second = moved(second, across)
    partner = moved(partner, other_core)
    total = add_compact(total, near)
    coarse, skel = skeletons(total, split, interp, cols, inverse_block, self_block)
    skel = moved(skel, other_core)
    coarse = place(coarse, skel)
    total = add_dense(total, partner, 0, 8)
    total = add_dense(total, second, FIRST, 4)
    total = add_dense(total, first, 0, 8)
    return total, coarse[None]


def solution(mesh):
    return jax.shard_map(
        body,
        mesh=mesh,
        in_specs=(
            P("box", None, None),
            P("box", None, None),
            P("box", None),
            P("box", None, None),
            P("box", None, None, None),
            P("box", None, None, None),
            P("box", None, None),
            P("box", None, None),
            P("box", None, None),
        ),
        out_specs=(P("box", None, None), P("box", None, None, None, None)),
        check_vma=False,
    )
```

```python
import functools

import jax
import jax.numpy as jnp
from jax import lax
from jax.experimental import pallas as pl
from jax.experimental.pallas import tpu as pltpu
from jax.sharding import PartitionSpec as P

P_SIZE = 512
SK = 128
RD = 384
BOXES = 2
NB = 8
PAIRS = 24
SLOTS = 48
CAP = 32
ROWS = NB * SK
TILE = 512
NEAR = 24
OVER = CAP - NEAR
PART = 16
TAILS = (2, 4, 6, 8, 12, 24)
MARK = 64
HEAD = 8
VMEM_BYTES = 65_200_000
F32 = jnp.float32
BF16 = jnp.bfloat16
NT = (((1,), (1,)), ((), ()))

ANY = pl.BlockSpec(memory_space=pl.ANY)
SMEM = pl.BlockSpec(memory_space=pltpu.SMEM)


def block_type(count):
    return jax.ShapeDtypeStruct((count, SK, SK), F32)


def cost(us):
    return pl.CostEstimate(flops=us * 1_000_000_000, bytes_accessed=0, transcendentals=0)


def payload_type(count):
    return jax.ShapeDtypeStruct((HEAD + count * SK, SK), F32)


def input_copies(hbm, vmem, sems):
    out = []
    for box in range(BOXES):
        out.append([
            pltpu.make_async_copy(source.at[box], target.at[box], sems.at[box, n])
            for n, (source, target) in enumerate(zip(hbm, vmem))
        ])
    return out


def compressor_of(split, interp, box):
    points = lax.broadcasted_iota(jnp.int32, (P_SIZE, RD), 0)
    pick_red = points == split[box:box + 1, :RD]
    points = lax.broadcasted_iota(jnp.int32, (P_SIZE, SK), 0)
    pick_skel = (points == split[box:box + 1, RD:]).astype(F32).astype(BF16)
    spread = lax.dot_general(pick_skel, interp[box], NT, preferred_element_type=F32)
    return (jnp.where(pick_red, 1.0, 0.0) - spread).astype(BF16), pick_skel


def mul(a, b):
    return jnp.dot(a, b, preferred_element_type=F32)


def products(box, copies, split, interp, inverse, rows, cols, w_far, y_near, compressor, grams):
    copies[0].wait()
    comp, pick_skel = compressor_of(split, interp, box)
    compressor[...] = comp
    copies[1].wait()

    def far(n, _):
        at = pl.ds(pl.multiple_of(n * TILE, TILE), TILE)
        w_far[at, :] = mul(cols[box, at, :], compressor[...]).astype(BF16)
        return 0

    lax.fori_loop(0, ROWS // TILE, far, 0, unroll=True)
    copies[2].wait()
    copies[3].wait()

    def near(n, _):
        at = pl.ds(pl.multiple_of(n * TILE, TILE), TILE)
        x_near = mul(rows[box, at, :], compressor[...]).astype(BF16)
        y_near[at, :] = mul(x_near, inverse[box]).astype(BF16)
        return 0

    lax.fori_loop(0, ROWS // TILE, near, 0, unroll=True)

    def gram(n, _):
        at = pl.ds(pl.multiple_of(n * TILE, TILE), TILE)
        tile = lax.dot_general(y_near[...], w_far[at, :], NT, preferred_element_type=F32)
        for i in range(NB):
            for k in range(TILE // SK):
                grams[i, n * (TILE // SK) + k] = tile[i * SK:(i + 1) * SK, k * SK:(k + 1) * SK]
        return 0

    lax.fori_loop(0, ROWS // TILE, gram, 0, unroll=True)
    return pick_skel


def block(n):
    return pl.ds(pl.multiple_of(n * SK, SK), SK)


def payload_block(n):
    return pl.ds(pl.multiple_of(HEAD + n * SK, 8), SK)


def work_list(targets, pairs, todo, used, places, first_touch):
    device = lax.axis_index("box")
    odd = lax.rem(device, 2) == 1
    all_slots = lax.axis_size("box") * SLOTS
    here = device * SLOTS
    ends = []
    for box in range(BOXES):

        def enter(pair, end):
            numbers = [pairs[box, 0, pair], pairs[box, 1, pair]]
            for side in range(2):
                away = targets[box, side, pair] - here
                away = jnp.where(away >= all_slots // 2, away - all_slots, away)
                away = jnp.where(away < -(all_slots // 2), away + all_slots, away)
                hops = jnp.int32(-2)
                for low in range(-1, 3):
                    hops = hops + (away >= low * SLOTS).astype(jnp.int32)
                slot = away - hops * SLOTS
                hops = jnp.where(odd, hops, -hops)
                place = jnp.int32(len(places) * SLOTS)
                for n, want in enumerate(places):
                    place = jnp.where(hops == want, slot + n * SLOTS, place)
                entry = place * 128 + numbers[side] * 16 + numbers[1 - side] * 2
                if first_touch:
                    entry = entry + used[place]
                    used[place] = 1
                todo[box, end] = entry
                end = end + (place < len(places) * SLOTS).astype(jnp.int32)
            return end

        ends.append(lax.fori_loop(0, PAIRS, enter, jnp.int32(0), unroll=2))
    return ends


def listed(entry):
    return lax.shift_right_logical(entry, 7), lax.shift_right_logical(entry, 4) & 7, lax.shift_right_logical(entry, 1) & 7


def front_kernel(targets_h, pairs_h, split_h, interp_h, cols_h, rows_h, inverse_h,
                 near_out, over_out, far_out, edge_out, partner_out,
                 interp, cols, rows, inverse, w_far, y_near, compressor, grams, split, acc, targets, pairs, todo, used,
                 near_head, far_head, edge_head, partner_head, in_sems, out_sems, small_sems):
    small = [
        pltpu.make_async_copy(targets_h, targets, small_sems.at[0]),
        pltpu.make_async_copy(pairs_h, pairs, small_sems.at[1]),
        pltpu.make_async_copy(split_h, split, small_sems.at[2]),
    ]
    for copy in small:
        copy.start()
    copies = input_copies((interp_h, cols_h, rows_h, inverse_h), (interp, cols, rows, inverse), in_sems)
    for box in range(BOXES):
        for copy in copies[box]:
            copy.start()

    def clear_used(n, _):
        used[n] = 0
        return 0

    lax.fori_loop(0, 4 * SLOTS, clear_used, 0, unroll=8)
    for copy in small:
        copy.wait()
    ends = work_list(targets, pairs, todo, used, (2, -2, 1, -1), True)

    def number(n, counts):
        name = n.astype(F32)
        near_head[0, counts[0]] = name
        edge_head[1, counts[0]] = name
        far_head[0, counts[1]] = name
        edge_head[0, counts[2]] = name
        partner_head[0, counts[3]] = name
        return tuple(count + used[base * SLOTS + n] for base, count in enumerate(counts))

    counts = lax.fori_loop(0, SLOTS, number, (jnp.int32(0),) * 4, unroll=4)
    rows_of = (near_head.at[0], far_head.at[0], edge_head.at[0], partner_head.at[0], edge_head.at[1])
    for row, count in zip(rows_of, (*counts, counts[0])):

        def blank(n, _):
            row[n] = -1.0
            return 0

        lax.fori_loop(count, CAP, blank, 0)

    for box in range(BOXES):
        products(box, copies[box], split, interp, inverse, rows, cols, w_far, y_near, compressor, grams)

        def add(n, _):
            entry = todo[box, n]
            place, i, j = listed(entry)
            acc[place] = jnp.where((entry & 1) == 1, acc[place], 0.0) - grams[i, j]
            return 0

        lax.fori_loop(0, ends[box], add, 0)

    labels = [
        pltpu.make_async_copy(near_head, near_out.at[pl.ds(0, HEAD)], small_sems.at[0]),
        pltpu.make_async_copy(far_head, far_out.at[pl.ds(0, HEAD)], small_sems.at[1]),
        pltpu.make_async_copy(edge_head, edge_out.at[pl.ds(0, HEAD)], small_sems.at[2]),
        pltpu.make_async_copy(partner_head, partner_out.at[pl.ds(0, HEAD)], small_sems.at[3]),
    ]
    for copy in labels:
        copy.start()
    near_count = jnp.minimum(counts[0], NEAR)
    lots = (
        (0, near_head, near_out, 0, near_count),
        (0, near_head, over_out, NEAR, counts[0]),
        (1, far_head, far_out, 0, counts[1]),
        (2, edge_head, edge_out, 0, counts[2]),
        (3, partner_head, partner_out, 0, counts[3]),
    )
    for base, head, out, begin, end in lots:

        def send(n, _):
            source = acc.at[base * SLOTS + head[0, n].astype(jnp.int32)]
            rows_at = block(n - begin) if begin else payload_block(n)
            pltpu.make_async_copy(source, out.at[rows_at], out_sems.at[base, n]).start()
            return 0

        lax.fori_loop(begin, end, send, 0)
    for base in range(4):

        def drain(n, _):
            pltpu.make_async_copy(acc.at[base], far_out.at[payload_block(0)], out_sems.at[base, n]).wait()
            return 0

        lax.fori_loop(0, counts[base], drain, 0)
    for copy in labels:
        copy.wait()


def box_scratch():
    return [
        pltpu.VMEM((BOXES, RD, SK), BF16),
        pltpu.VMEM((BOXES, ROWS, P_SIZE), BF16),
        pltpu.VMEM((BOXES, ROWS, P_SIZE), BF16),
        pltpu.VMEM((BOXES, RD, RD), BF16),
        pltpu.VMEM((ROWS, RD), BF16),
        pltpu.VMEM((ROWS, RD), BF16),
        pltpu.VMEM((P_SIZE, RD), BF16),
        pltpu.VMEM((NB, NB, SK, SK), F32),
    ]


def front(targets, pairs, split, interp, cols, rows, inverse):
    return pl.pallas_call(
        front_kernel,
        out_shape=(
            payload_type(NEAR), jax.ShapeDtypeStruct((OVER * SK, SK), F32),
            payload_type(CAP), payload_type(CAP), payload_type(CAP),
        ),
        in_specs=[ANY] * 7,
        out_specs=(ANY,) * 5,
        scratch_shapes=box_scratch() + [
            pltpu.VMEM((BOXES, P_SIZE), jnp.int32),
            pltpu.VMEM((4 * SLOTS + 1, SK, SK), F32),
            pltpu.SMEM((BOXES, 2, PAIRS), jnp.int32),
            pltpu.SMEM((BOXES, 2, PAIRS), jnp.int32),
            pltpu.SMEM((BOXES, 2 * PAIRS + 1), jnp.int32),
            pltpu.SMEM((4 * SLOTS + 1,), jnp.int32),
            pltpu.SMEM((HEAD, 128), F32),
            pltpu.SMEM((HEAD, 128), F32),
            pltpu.SMEM((HEAD, 128), F32),
            pltpu.SMEM((HEAD, 128), F32),
            pltpu.SemaphoreType.DMA((BOXES, 4)),
            pltpu.SemaphoreType.DMA((4, CAP)),
            pltpu.SemaphoreType.DMA((4,)),
        ],
        compiler_params=pltpu.CompilerParams(vmem_limit_bytes=VMEM_BYTES),
        cost_estimate=cost(1),
        name="front",
    )(targets, pairs, split, interp, cols, rows, inverse)


def rest_kernel(targets_h, pairs_h, split_h, interp_h, cols_h, rows_h, inverse_h, self_h, start_h,
                total_out, coarse_out, skel_out,
                interp, cols, rows, inverse, self_block, w_far, y_near, compressor, grams, split, start, acc, skel,
                targets, pairs, todo, in_sems, out_sems, small_sems):
    small = [
        pltpu.make_async_copy(targets_h, targets, small_sems.at[0]),
        pltpu.make_async_copy(pairs_h, pairs, small_sems.at[1]),
        pltpu.make_async_copy(split_h, split, small_sems.at[2]),
    ]
    for copy in small:
        copy.start()
    copies = input_copies((interp_h, cols_h, rows_h, inverse_h, self_h), (interp, cols, rows, inverse, self_block), in_sems)
    start_copy = pltpu.make_async_copy(start_h, start, out_sems.at[4])
    for copy in copies[0]:
        copy.start()
    start_copy.start()
    for copy in copies[1]:
        copy.start()

    for copy in small:
        copy.wait()
    ends = work_list(targets, pairs, todo, None, (0,), False)
    start_copy.wait()

    def widen(n, _):
        acc[n] = start[n].astype(F32)
        return 0

    lax.fori_loop(0, SLOTS, widen, 0)
    parity = lax.rem(lax.axis_index("box"), 2)
    for box in range(BOXES):
        pick_skel = products(box, copies[box], split, interp, inverse, rows, cols, w_far, y_near, compressor, grams)

        def add(n, _):
            place, i, j = listed(todo[box, n])
            acc[place] = acc[place] - grams[i, j]
            return 0

        lax.fori_loop(0, ends[box], add, 0)
        copies[box][4].wait()
        x_self = mul(self_block[box], compressor[...]).astype(BF16)
        y_self = mul(x_self, inverse[box]).astype(BF16)
        pick_rows = pick_skel.astype(F32).T.astype(BF16)
        for n in range(ROWS // TILE):
            at = slice(n * TILE, (n + 1) * TILE)
            base = lax.dot_general(pick_rows, cols[box, at, :], NT, preferred_element_type=F32)
            base = base - lax.dot_general(y_self, w_far[at, :], NT, preferred_element_type=F32)
            for k in range(TILE // SK):
                j = n * (TILE // SK) + k
                skel[j // 4, box, j % 4] = base[:, k * SK:(k + 1) * SK]

    outs = [
        pltpu.make_async_copy(acc, total_out, out_sems.at[1]),
        pltpu.make_async_copy(skel.at[parity], coarse_out.at[pl.ds(2 * parity, 2)], out_sems.at[2]),
        pltpu.make_async_copy(skel.at[1 - parity], skel_out, out_sems.at[3]),
    ]
    for copy in outs:
        copy.start()
    for copy in outs:
        copy.wait()


def rest(targets, pairs, split, interp, cols, rows, inverse, self_block, start):
    scratch = box_scratch()
    scratch.insert(4, pltpu.VMEM((BOXES, SK, P_SIZE), BF16))
    return pl.pallas_call(
        rest_kernel,
        out_shape=(
            block_type(SLOTS),
            jax.ShapeDtypeStruct((2 * BOXES, NB // 2, SK, SK), F32),
            jax.ShapeDtypeStruct((BOXES, NB // 2, SK, SK), F32),
        ),
        in_specs=[ANY] * 9,
        out_specs=(ANY,) * 3,
        scratch_shapes=scratch + [
            pltpu.VMEM((BOXES, P_SIZE), jnp.int32),
            pltpu.VMEM((SLOTS, SK, SK), BF16),
            pltpu.VMEM((SLOTS, SK, SK), F32),
            pltpu.VMEM((2, BOXES, NB // 2, SK, SK), F32),
            pltpu.SMEM((BOXES, 2, PAIRS), jnp.int32),
            pltpu.SMEM((BOXES, 2, PAIRS), jnp.int32),
            pltpu.SMEM((BOXES, 2 * PAIRS + 1), jnp.int32),
            pltpu.SemaphoreType.DMA((BOXES, 5)),
            pltpu.SemaphoreType.DMA((5,)),
            pltpu.SemaphoreType.DMA((3,)),
        ],
        compiler_params=pltpu.CompilerParams(vmem_limit_bytes=VMEM_BYTES),
        cost_estimate=cost(1),
        name="rest",
    )(targets, pairs, split, interp, cols, rows, inverse, self_block, start)


def merge_kernel(over_h, edge_h, far_h, first_out, second_out, *refs):
    tail_outs = refs[:len(TAILS)]
    tail_count, blocks, edge_head, far_head, head, places, sources, in_sems, out_sems, tail_sems = refs[len(TAILS):]
    heads = [
        pltpu.make_async_copy(edge_h.at[pl.ds(0, HEAD)], edge_head, in_sems.at[0]),
        pltpu.make_async_copy(far_h.at[pl.ds(0, HEAD)], far_head, in_sems.at[1]),
    ]
    bulk = [
        pltpu.make_async_copy(over_h, blocks.at[pl.ds(0, OVER * SK)], in_sems.at[2]),
        pltpu.make_async_copy(edge_h.at[pl.ds(HEAD, CAP * SK)], blocks.at[pl.ds(OVER * SK, CAP * SK)], in_sems.at[3]),
        pltpu.make_async_copy(far_h.at[pl.ds(HEAD, CAP * SK)], blocks.at[pl.ds((OVER + CAP) * SK, CAP * SK)], in_sems.at[4]),
    ]
    for copy in heads + bulk:
        copy.start()

    def clear(n, _):
        places[n] = -1
        return 0

    lax.fori_loop(0, SLOTS, clear, 0, unroll=8)
    for copy in heads:
        copy.wait()

    def take_over(n, count):
        slot = edge_head[1, NEAR + n]
        head[0, count] = slot + MARK
        sources[count] = n
        return count + (slot >= 0.0).astype(jnp.int32)

    count = lax.fori_loop(0, OVER, take_over, jnp.int32(0))

    def take_edge(n, count):
        slot = edge_head[0, n]
        found = slot >= 0.0
        head[0, count] = slot
        sources[count] = OVER + n

        @pl.when(found)
        def _():
            places[slot.astype(jnp.int32)] = OVER + n

        return count + found.astype(jnp.int32)

    count = lax.fori_loop(0, CAP, take_edge, count)
    for copy in bulk:
        copy.wait()

    def take_far(n, count):
        slot = far_head[0, n]
        found = slot >= 0.0
        place = places[jnp.maximum(slot.astype(jnp.int32), 0)]
        head[0, count] = slot
        sources[count] = OVER + CAP + n

        @pl.when(found & (place >= 0))
        def _():
            blocks[block(place), :] = blocks[block(place), :] + blocks[block(OVER + CAP + n), :]

        return count + (found & (place < 0)).astype(jnp.int32)

    count = lax.fori_loop(0, CAP, take_far, count)

    def blank(n, _):
        head[0, n] = -1.0
        return 0

    lax.fori_loop(count, SLOTS + OVER, blank, 0)
    left = jnp.maximum(count - 2 * PART, 0)
    tail_count[0] = left
    head[1, 0] = left.astype(F32)
    label = pltpu.make_async_copy(head, first_out.at[pl.ds(0, HEAD)], in_sems.at[0])
    label.start()

    def send_first(n, _):
        pltpu.make_async_copy(blocks.at[block(sources[n])], first_out.at[payload_block(n)], out_sems.at[n]).start()
        return 0

    def send_second(n, _):
        pltpu.make_async_copy(blocks.at[block(sources[n])], second_out.at[block(n - PART)], out_sems.at[n]).start()
        return 0

    lax.fori_loop(0, jnp.minimum(count, PART), send_first, 0)
    lax.fori_loop(PART, jnp.minimum(count, 2 * PART), send_second, 0)

    def send_tail(n, _):
        for k, (size, out) in enumerate(zip(TAILS, tail_outs)):

            @pl.when(left <= size)
            def _():
                source = blocks.at[block(sources[2 * PART + n])]
                pltpu.make_async_copy(source, out.at[block(n)], tail_sems.at[k, n]).start()

        return 0

    lax.fori_loop(0, left, send_tail, 0)

    def drain(n, _):
        pltpu.make_async_copy(blocks.at[block(0)], second_out.at[block(0)], out_sems.at[n]).wait()
        return 0

    lax.fori_loop(0, jnp.minimum(count, 2 * PART), drain, 0)

    def drain_tail(n, _):
        for k, size in enumerate(TAILS):

            @pl.when(left <= size)
            def _():
                pltpu.make_async_copy(blocks.at[block(0)], second_out.at[block(0)], tail_sems.at[k, n]).wait()

        return 0

    lax.fori_loop(0, left, drain_tail, 0)
    label.wait()


def merge(over, edge, far):
    return pl.pallas_call(
        merge_kernel,
        out_shape=(
            payload_type(PART),
            jax.ShapeDtypeStruct((PART * SK, SK), F32),
            *[jax.ShapeDtypeStruct((size * SK, SK), F32) for size in TAILS],
            jax.ShapeDtypeStruct((1,), jnp.int32),
        ),
        in_specs=[ANY] * 3,
        out_specs=(ANY,) * (2 + len(TAILS)) + (SMEM,),
        scratch_shapes=[
            pltpu.VMEM(((OVER + 2 * CAP) * SK, SK), F32),
            pltpu.SMEM((HEAD, 128), F32),
            pltpu.SMEM((HEAD, 128), F32),
            pltpu.SMEM((HEAD, 128), F32),
            pltpu.SMEM((SLOTS,), jnp.int32),
            pltpu.SMEM((SLOTS + OVER + 1,), jnp.int32),
            pltpu.SemaphoreType.DMA((5,)),
            pltpu.SemaphoreType.DMA((2 * PART,)),
            pltpu.SemaphoreType.DMA((len(TAILS), TAILS[-1])),
        ],
        compiler_params=pltpu.CompilerParams(vmem_limit_bytes=VMEM_BYTES),
        cost_estimate=cost(1),
        name="merge",
    )(over, edge, far)


def add_early_kernel(own_count, total_h, near_h, partner_h, first_h, out, branch,
                     total, near, partner, first, near_head, partner_head, first_head, sems):
    copies = [
        pltpu.make_async_copy(near_h.at[pl.ds(0, HEAD)], near_head, sems.at[0]),
        pltpu.make_async_copy(first_h.at[pl.ds(0, HEAD)], first_head, sems.at[1]),
        pltpu.make_async_copy(near_h.at[pl.ds(HEAD, NEAR * SK)], near, sems.at[2]),
        pltpu.make_async_copy(first_h.at[pl.ds(HEAD, PART * SK)], first, sems.at[3]),
        pltpu.make_async_copy(total_h, total, sems.at[4]),
        pltpu.make_async_copy(partner_h.at[pl.ds(0, HEAD)], partner_head, sems.at[5]),
        pltpu.make_async_copy(partner_h.at[pl.ds(HEAD, CAP * SK)], partner, sems.at[6]),
    ]
    for copy in copies:
        copy.start()
    for copy in copies:
        copy.wait()
    left = jnp.maximum(own_count[0], first_head[1, 0].astype(jnp.int32))
    which = jnp.int32(0)
    for size in (0, *TAILS[:-1]):
        which = which + (left > size).astype(jnp.int32)
    branch[0] = which
    for head, blocks, count in ((near_head, near, NEAR), (partner_head, partner, CAP), (first_head, first, PART)):

        def add(n, _):
            slot = head[0, n].astype(jnp.int32)

            @pl.when((slot >= 0) & (slot < SLOTS))
            def _():
                total[slot] = total[slot] + blocks[block(n), :]

            return 0

        lax.fori_loop(0, count, add, 0)
    copy = pltpu.make_async_copy(total, out, sems.at[0])
    copy.start()
    copy.wait()


def add_early(own_count, total, near, partner, first):
    return pl.pallas_call(
        add_early_kernel,
        out_shape=(block_type(SLOTS), jax.ShapeDtypeStruct((1,), jnp.int32)),
        in_specs=[SMEM] + [ANY] * 4,
        out_specs=(ANY, SMEM),
        scratch_shapes=[
            pltpu.VMEM((SLOTS, SK, SK), F32),
            pltpu.VMEM((NEAR * SK, SK), F32),
            pltpu.VMEM((CAP * SK, SK), F32),
            pltpu.VMEM((PART * SK, SK), F32),
            pltpu.SMEM((HEAD, 128), F32),
            pltpu.SMEM((HEAD, 128), F32),
            pltpu.SMEM((HEAD, 128), F32),
            pltpu.SemaphoreType.DMA((7,)),
        ],
        input_output_aliases={1: 0},
        compiler_params=pltpu.CompilerParams(vmem_limit_bytes=VMEM_BYTES),
        cost_estimate=cost(1),
        name="add_early",
    )(own_count, total, near, partner, first)


def add_late_kernel(begin, base, skip, total_h, first_h, blocks_h, out, total, blocks, head, sems, slot_sems):
    count = total.shape[0]
    names = pltpu.make_async_copy(first_h.at[pl.ds(0, HEAD)], head, sems.at[0])
    bulk = pltpu.make_async_copy(blocks_h.at[pl.ds(skip, count * SK)], blocks, sems.at[1])
    names.start()
    bulk.start()
    names.wait()

    def each(act):
        def step(n, _):
            slot = head[0, begin + n].astype(jnp.int32) - base

            @pl.when((slot >= 0) & (slot < SLOTS))
            def _():
                act(n, slot)

            return 0

        lax.fori_loop(0, count, step, 0)

    def load(n, slot):
        pltpu.make_async_copy(total_h.at[slot], total.at[n], slot_sems.at[0, n]).start()

    def add(n, slot):
        pltpu.make_async_copy(total_h.at[slot], total.at[n], slot_sems.at[0, n]).wait()
        total[n] = total[n] + blocks[block(n), :]
        pltpu.make_async_copy(total.at[n], out.at[slot], slot_sems.at[1, n]).start()

    def drain(n, slot):
        pltpu.make_async_copy(total.at[n], out.at[slot], slot_sems.at[1, n]).wait()

    each(load)
    bulk.wait()
    each(add)
    each(drain)


def add_late(total, first, blocks, begin, base=0, skip=0):
    count = blocks.shape[0] // SK
    return pl.pallas_call(
        functools.partial(add_late_kernel, begin, base, skip),
        out_shape=block_type(SLOTS),
        in_specs=[ANY] * 3,
        out_specs=ANY,
        scratch_shapes=[
            pltpu.VMEM((count, SK, SK), F32),
            pltpu.VMEM((count * SK, SK), F32),
            pltpu.SMEM((HEAD, 128), F32),
            pltpu.SemaphoreType.DMA((2,)),
            pltpu.SemaphoreType.DMA((2, count)),
        ],
        input_output_aliases={0: 0},
        compiler_params=pltpu.CompilerParams(vmem_limit_bytes=VMEM_BYTES),
        cost_estimate=cost(1),
        name="add_late",
    )(total, first, blocks)


def place_kernel(coarse, received, out, held, sems):
    parity = lax.rem(lax.axis_index("box"), 2)
    copy = pltpu.make_async_copy(received, held, sems.at[0])
    copy.start()
    copy.wait()
    copy = pltpu.make_async_copy(held, out.at[pl.ds(2 - 2 * parity, 2)], sems.at[1])
    copy.start()
    copy.wait()


def place(coarse, received):
    return pl.pallas_call(
        place_kernel,
        out_shape=jax.ShapeDtypeStruct(coarse.shape, F32),
        in_specs=[ANY, ANY],
        out_specs=ANY,
        scratch_shapes=[pltpu.VMEM((BOXES, NB // 2, SK, SK), F32), pltpu.SemaphoreType.DMA((2,))],
        input_output_aliases={0: 0},
        compiler_params=pltpu.CompilerParams(vmem_limit_bytes=VMEM_BYTES),
        cost_estimate=cost(1),
        name="place",
    )(coarse, received)


def moved(value, route):
    devices = lax.axis_size("box")
    return lax.ppermute(value, "box", [(i, route(i) % devices) for i in range(devices)])


def other_core(i):
    return i ^ 1


def across(i):
    return i + 1 if i % 2 else i - 1


def beyond(i):
    return i + 2 if i % 2 else i - 2


def body(self_block, interp, split, inverse_block, row_blocks, col_blocks, pairs, targets, pair_blocks):
    targets = jnp.transpose(targets, (0, 2, 1))
    pairs = jnp.transpose(pairs, (0, 2, 1))
    rows = row_blocks.reshape(BOXES, ROWS, P_SIZE)
    cols = col_blocks.reshape(BOXES, ROWS, P_SIZE)
    near, over, far, edge, partner = front(targets, pairs, split, interp, cols, rows, inverse_block)
    near = moved(near, beyond)
    far = moved(far, other_core)
    partner = moved(partner, other_core)
    first, second, *tails, own_count = merge(over, edge, far)
    total, coarse, skel = rest(targets, pairs, split, interp, cols, rows, inverse_block, self_block, pair_blocks)
    first = moved(first, across)
    second = moved(second, across)
    skel = moved(skel, other_core)
    coarse = place(coarse, skel)
    total, branch = add_early(own_count, total, near, partner, first)
    forward = moved(first[:HEAD + OVER * SK], other_core)
    total = add_late(total, forward, forward, 0, MARK, HEAD)

    def none(total, first, second, *tails):
        return add_late(total, first, second, PART)

    def some(which):
        def send(total, first, second, *tails):
            tail = moved(tails[which], across)
            total = add_late(total, first, second, PART)
            return add_late(total, first, tail, 2 * PART)

        return send

    branches = [none] + [some(n) for n in range(len(TAILS))]
    total = lax.switch(branch[0], branches, total, first, second, *tails)
    return total, coarse[None]


def solution(mesh):
    return jax.shard_map(
        body,
        mesh=mesh,
        in_specs=(
            P("box", None, None),
            P("box", None, None),
            P("box", None),
            P("box", None, None),
            P("box", None, None, None),
            P("box", None, None, None),
            P("box", None, None),
            P("box", None, None),
            P("box", None, None),
        ),
        out_specs=(P("box", None, None), P("box", None, None, None, None)),
        check_vma=False,
    )
```

```python
import functools

import jax
import jax.numpy as jnp
from jax import lax
from jax.experimental import pallas as pl
from jax.experimental.pallas import tpu as pltpu
from jax.sharding import PartitionSpec as P

P_SIZE = 512
SK = 128
RD = 384
BOXES = 2
NB = 8
PAIRS = 24
SLOTS = 48
CAP = 32
ROWS = NB * SK
TILE = 512
NEAR = 20
OVER = CAP - NEAR
PART = 12
SECOND = 20
FIXED = PART + SECOND
TAILS = (3, 5, 7, 9, 12, 28)
MARK = 64
PARCELS = ((NEAR, 0), (CAP, 0), (PART, 0), (OVER, MARK))
HEAD = 8
VMEM_BYTES = 65_200_000
F32 = jnp.float32
BF16 = jnp.bfloat16
NT = (((1,), (1,)), ((), ()))

ANY = pl.BlockSpec(memory_space=pl.ANY)
SMEM = pl.BlockSpec(memory_space=pltpu.SMEM)


def block_type(count):
    return jax.ShapeDtypeStruct((count, SK, SK), F32)


def cost(us):
    return pl.CostEstimate(flops=us * 1_000_000_000, bytes_accessed=0, transcendentals=0)


def payload_type(count):
    return jax.ShapeDtypeStruct((HEAD + count * SK, SK), F32)


def input_copies(hbm, vmem, sems):
    out = []
    for box in range(BOXES):
        out.append([
            pltpu.make_async_copy(source.at[box], target.at[box], sems.at[box, n])
            for n, (source, target) in enumerate(zip(hbm, vmem))
        ])
    return out


def compressor_of(split, interp, box):
    points = lax.broadcasted_iota(jnp.int32, (P_SIZE, RD), 0)
    pick_red = points == split[box:box + 1, :RD]
    points = lax.broadcasted_iota(jnp.int32, (P_SIZE, SK), 0)
    pick_skel = (points == split[box:box + 1, RD:]).astype(F32).astype(BF16)
    spread = lax.dot_general(pick_skel, interp[box], NT, preferred_element_type=F32)
    return (jnp.where(pick_red, 1.0, 0.0) - spread).astype(BF16), pick_skel


def mul(a, b):
    return jnp.dot(a, b, preferred_element_type=F32)


def products(box, copies, split, interp, inverse, rows, cols, w_far, y_near, compressor, grams):
    copies[0].wait()
    comp, pick_skel = compressor_of(split, interp, box)
    compressor[...] = comp
    copies[1].wait()

    def far(n, _):
        at = pl.ds(pl.multiple_of(n * TILE, TILE), TILE)
        w_far[at, :] = mul(cols[box, at, :], compressor[...]).astype(BF16)
        return 0

    lax.fori_loop(0, ROWS // TILE, far, 0, unroll=True)
    copies[2].wait()
    copies[3].wait()

    def near(n, _):
        at = pl.ds(pl.multiple_of(n * TILE, TILE), TILE)
        x_near = mul(rows[box, at, :], compressor[...]).astype(BF16)
        y_near[at, :] = mul(x_near, inverse[box]).astype(BF16)
        return 0

    lax.fori_loop(0, ROWS // TILE, near, 0, unroll=True)

    def gram(n, _):
        at = pl.ds(pl.multiple_of(n * TILE, TILE), TILE)
        tile = lax.dot_general(y_near[...], w_far[at, :], NT, preferred_element_type=F32)
        for i in range(NB):
            for k in range(TILE // SK):
                grams[i, n * (TILE // SK) + k] = tile[i * SK:(i + 1) * SK, k * SK:(k + 1) * SK]
        return 0

    lax.fori_loop(0, ROWS // TILE, gram, 0, unroll=True)
    return pick_skel


def block(n):
    return pl.ds(pl.multiple_of(n * SK, SK), SK)


def payload_block(n):
    return pl.ds(pl.multiple_of(HEAD + n * SK, 8), SK)


def work_list(targets, pairs, todo, used, places, first_touch):
    device = lax.axis_index("box")
    odd = lax.rem(device, 2) == 1
    all_slots = lax.axis_size("box") * SLOTS
    here = device * SLOTS
    ends = []
    for box in range(BOXES):

        def enter(pair, end):
            numbers = [pairs[box, 0, pair], pairs[box, 1, pair]]
            for side in range(2):
                away = targets[box, side, pair] - here
                away = jnp.where(away >= all_slots // 2, away - all_slots, away)
                away = jnp.where(away < -(all_slots // 2), away + all_slots, away)
                hops = jnp.int32(-2)
                for low in range(-1, 3):
                    hops = hops + (away >= low * SLOTS).astype(jnp.int32)
                slot = away - hops * SLOTS
                hops = jnp.where(odd, hops, -hops)
                place = jnp.int32(len(places) * SLOTS)
                for n, want in enumerate(places):
                    place = jnp.where(hops == want, slot + n * SLOTS, place)
                entry = place * 128 + numbers[side] * 16 + numbers[1 - side] * 2
                if first_touch:
                    entry = entry + used[place]
                    used[place] = 1
                todo[box, end] = entry
                end = end + (place < len(places) * SLOTS).astype(jnp.int32)
            return end

        ends.append(lax.fori_loop(0, PAIRS, enter, jnp.int32(0), unroll=2))
    return ends


def listed(entry):
    return lax.shift_right_logical(entry, 7), lax.shift_right_logical(entry, 4) & 7, lax.shift_right_logical(entry, 1) & 7


def front_kernel(targets_h, pairs_h, split_h, interp_h, cols_h, rows_h, inverse_h,
                 near_out, over_out, far_out, edge_out, partner_out,
                 interp, cols, rows, inverse, w_far, y_near, compressor, grams, split, acc, targets, pairs, todo, used,
                 near_head, far_head, edge_head, partner_head, in_sems, out_sems, small_sems):
    small = [
        pltpu.make_async_copy(targets_h, targets, small_sems.at[0]),
        pltpu.make_async_copy(pairs_h, pairs, small_sems.at[1]),
        pltpu.make_async_copy(split_h, split, small_sems.at[2]),
    ]
    for copy in small:
        copy.start()
    copies = input_copies((interp_h, cols_h, rows_h, inverse_h), (interp, cols, rows, inverse), in_sems)
    for box in range(BOXES):
        for copy in copies[box]:
            copy.start()

    def clear_used(n, _):
        used[n] = 0
        return 0

    lax.fori_loop(0, 4 * SLOTS, clear_used, 0, unroll=8)
    for copy in small:
        copy.wait()
    ends = work_list(targets, pairs, todo, used, (2, -2, 1, -1), True)

    def number(n, counts):
        name = n.astype(F32)
        near_head[0, counts[0]] = name
        edge_head[1, counts[0]] = name
        far_head[0, counts[1]] = name
        edge_head[0, counts[2]] = name
        partner_head[0, counts[3]] = name
        return tuple(count + used[base * SLOTS + n] for base, count in enumerate(counts))

    counts = lax.fori_loop(0, SLOTS, number, (jnp.int32(0),) * 4, unroll=4)
    rows_of = (near_head.at[0], far_head.at[0], edge_head.at[0], partner_head.at[0], edge_head.at[1])
    for row, count in zip(rows_of, (*counts, counts[0])):

        def blank(n, _):
            row[n] = -1.0
            return 0

        lax.fori_loop(count, CAP, blank, 0)

    for box in range(BOXES):
        products(box, copies[box], split, interp, inverse, rows, cols, w_far, y_near, compressor, grams)

        def add(n, _):
            entry = todo[box, n]
            place, i, j = listed(entry)
            acc[place] = jnp.where((entry & 1) == 1, acc[place], 0.0) - grams[i, j]
            return 0

        lax.fori_loop(0, ends[box], add, 0)

    labels = [
        pltpu.make_async_copy(near_head, near_out.at[pl.ds(0, HEAD)], small_sems.at[0]),
        pltpu.make_async_copy(far_head, far_out.at[pl.ds(0, HEAD)], small_sems.at[1]),
        pltpu.make_async_copy(edge_head, edge_out.at[pl.ds(0, HEAD)], small_sems.at[2]),
        pltpu.make_async_copy(partner_head, partner_out.at[pl.ds(0, HEAD)], small_sems.at[3]),
    ]
    for copy in labels:
        copy.start()
    near_count = jnp.minimum(counts[0], NEAR)
    lots = (
        (0, near_head, near_out, 0, near_count),
        (0, near_head, over_out, NEAR, counts[0]),
        (1, far_head, far_out, 0, counts[1]),
        (2, edge_head, edge_out, 0, counts[2]),
        (3, partner_head, partner_out, 0, counts[3]),
    )
    for base, head, out, begin, end in lots:

        def send(n, _):
            source = acc.at[base * SLOTS + head[0, n].astype(jnp.int32)]
            rows_at = block(n - begin) if begin else payload_block(n)
            pltpu.make_async_copy(source, out.at[rows_at], out_sems.at[base, n]).start()
            return 0

        lax.fori_loop(begin, end, send, 0)
    for base in range(4):

        def drain(n, _):
            pltpu.make_async_copy(acc.at[base], far_out.at[payload_block(0)], out_sems.at[base, n]).wait()
            return 0

        lax.fori_loop(0, counts[base], drain, 0)
    for copy in labels:
        copy.wait()


def box_scratch():
    return [
        pltpu.VMEM((BOXES, RD, SK), BF16),
        pltpu.VMEM((BOXES, ROWS, P_SIZE), BF16),
        pltpu.VMEM((BOXES, ROWS, P_SIZE), BF16),
        pltpu.VMEM((BOXES, RD, RD), BF16),
        pltpu.VMEM((ROWS, RD), BF16),
        pltpu.VMEM((ROWS, RD), BF16),
        pltpu.VMEM((P_SIZE, RD), BF16),
        pltpu.VMEM((NB, NB, SK, SK), F32),
    ]


def front(targets, pairs, split, interp, cols, rows, inverse):
    return pl.pallas_call(
        front_kernel,
        out_shape=(
            payload_type(NEAR), jax.ShapeDtypeStruct((OVER * SK, SK), F32),
            payload_type(CAP), payload_type(CAP), payload_type(CAP),
        ),
        in_specs=[ANY] * 7,
        out_specs=(ANY,) * 5,
        scratch_shapes=box_scratch() + [
            pltpu.VMEM((BOXES, P_SIZE), jnp.int32),
            pltpu.VMEM((4 * SLOTS + 1, SK, SK), F32),
            pltpu.SMEM((BOXES, 2, PAIRS), jnp.int32),
            pltpu.SMEM((BOXES, 2, PAIRS), jnp.int32),
            pltpu.SMEM((BOXES, 2 * PAIRS + 1), jnp.int32),
            pltpu.SMEM((4 * SLOTS + 1,), jnp.int32),
            pltpu.SMEM((HEAD, 128), F32),
            pltpu.SMEM((HEAD, 128), F32),
            pltpu.SMEM((HEAD, 128), F32),
            pltpu.SMEM((HEAD, 128), F32),
            pltpu.SemaphoreType.DMA((BOXES, 4)),
            pltpu.SemaphoreType.DMA((4, CAP)),
            pltpu.SemaphoreType.DMA((4,)),
        ],
        compiler_params=pltpu.CompilerParams(vmem_limit_bytes=VMEM_BYTES),
        cost_estimate=cost(1),
        name="front",
    )(targets, pairs, split, interp, cols, rows, inverse)


def rest_kernel(targets_h, pairs_h, split_h, interp_h, cols_h, rows_h, inverse_h, self_h, start_h,
                total_out, coarse_out, skel_out,
                interp, cols, rows, inverse, self_block, w_far, y_near, compressor, grams, split, start, acc, skel,
                targets, pairs, todo, in_sems, out_sems, small_sems):
    small = [
        pltpu.make_async_copy(targets_h, targets, small_sems.at[0]),
        pltpu.make_async_copy(pairs_h, pairs, small_sems.at[1]),
        pltpu.make_async_copy(split_h, split, small_sems.at[2]),
    ]
    for copy in small:
        copy.start()
    copies = input_copies((interp_h, cols_h, rows_h, inverse_h, self_h), (interp, cols, rows, inverse, self_block), in_sems)
    start_copy = pltpu.make_async_copy(start_h, start, out_sems.at[4])
    for copy in copies[0]:
        copy.start()
    start_copy.start()
    for copy in copies[1]:
        copy.start()

    for copy in small:
        copy.wait()
    ends = work_list(targets, pairs, todo, None, (0,), False)
    start_copy.wait()

    def widen(n, _):
        acc[n] = start[n].astype(F32)
        return 0

    lax.fori_loop(0, SLOTS, widen, 0)
    parity = lax.rem(lax.axis_index("box"), 2)
    for box in range(BOXES):
        pick_skel = products(box, copies[box], split, interp, inverse, rows, cols, w_far, y_near, compressor, grams)

        def add(n, _):
            place, i, j = listed(todo[box, n])
            acc[place] = acc[place] - grams[i, j]
            return 0

        lax.fori_loop(0, ends[box], add, 0)
        copies[box][4].wait()
        x_self = mul(self_block[box], compressor[...]).astype(BF16)
        y_self = mul(x_self, inverse[box]).astype(BF16)
        pick_rows = pick_skel.astype(F32).T.astype(BF16)
        for n in range(ROWS // TILE):
            at = slice(n * TILE, (n + 1) * TILE)
            base = lax.dot_general(pick_rows, cols[box, at, :], NT, preferred_element_type=F32)
            base = base - lax.dot_general(y_self, w_far[at, :], NT, preferred_element_type=F32)
            for k in range(TILE // SK):
                j = n * (TILE // SK) + k
                skel[j // 4, box, j % 4] = base[:, k * SK:(k + 1) * SK]

    outs = [
        pltpu.make_async_copy(acc, total_out, out_sems.at[1]),
        pltpu.make_async_copy(skel.at[parity], coarse_out.at[pl.ds(2 * parity, 2)], out_sems.at[2]),
        pltpu.make_async_copy(skel.at[1 - parity], skel_out, out_sems.at[3]),
    ]
    for copy in outs:
        copy.start()
    for copy in outs:
        copy.wait()


def rest(targets, pairs, split, interp, cols, rows, inverse, self_block, start):
    scratch = box_scratch()
    scratch.insert(4, pltpu.VMEM((BOXES, SK, P_SIZE), BF16))
    return pl.pallas_call(
        rest_kernel,
        out_shape=(
            block_type(SLOTS),
            jax.ShapeDtypeStruct((2 * BOXES, NB // 2, SK, SK), F32),
            jax.ShapeDtypeStruct((BOXES, NB // 2, SK, SK), F32),
        ),
        in_specs=[ANY] * 9,
        out_specs=(ANY,) * 3,
        scratch_shapes=scratch + [
            pltpu.VMEM((BOXES, P_SIZE), jnp.int32),
            pltpu.VMEM((SLOTS, SK, SK), BF16),
            pltpu.VMEM((SLOTS, SK, SK), F32),
            pltpu.VMEM((2, BOXES, NB // 2, SK, SK), F32),
            pltpu.SMEM((BOXES, 2, PAIRS), jnp.int32),
            pltpu.SMEM((BOXES, 2, PAIRS), jnp.int32),
            pltpu.SMEM((BOXES, 2 * PAIRS + 1), jnp.int32),
            pltpu.SemaphoreType.DMA((BOXES, 5)),
            pltpu.SemaphoreType.DMA((5,)),
            pltpu.SemaphoreType.DMA((3,)),
        ],
        compiler_params=pltpu.CompilerParams(vmem_limit_bytes=VMEM_BYTES),
        cost_estimate=cost(1),
        name="rest",
    )(targets, pairs, split, interp, cols, rows, inverse, self_block, start)


def merge_kernel(over_h, edge_h, far_h, first_out, second_out, *refs):
    tail_outs = refs[:len(TAILS)]
    tail_count, blocks, edge_head, far_head, head, places, sources, in_sems, out_sems, tail_sems = refs[len(TAILS):]
    heads = [
        pltpu.make_async_copy(edge_h.at[pl.ds(0, HEAD)], edge_head, in_sems.at[0]),
        pltpu.make_async_copy(far_h.at[pl.ds(0, HEAD)], far_head, in_sems.at[1]),
    ]
    bulk = [
        pltpu.make_async_copy(over_h, blocks.at[pl.ds(0, OVER * SK)], in_sems.at[2]),
        pltpu.make_async_copy(edge_h.at[pl.ds(HEAD, CAP * SK)], blocks.at[pl.ds(OVER * SK, CAP * SK)], in_sems.at[3]),
        pltpu.make_async_copy(far_h.at[pl.ds(HEAD, CAP * SK)], blocks.at[pl.ds((OVER + CAP) * SK, CAP * SK)], in_sems.at[4]),
    ]
    for copy in heads + bulk:
        copy.start()

    def clear(n, _):
        places[n] = -1
        return 0

    lax.fori_loop(0, SLOTS, clear, 0, unroll=8)
    for copy in heads:
        copy.wait()

    def take_over(n, count):
        slot = edge_head[1, NEAR + n]
        head[0, count] = slot + MARK
        sources[count] = n
        return count + (slot >= 0.0).astype(jnp.int32)

    count = lax.fori_loop(0, OVER, take_over, jnp.int32(0))

    def take_edge(n, count):
        slot = edge_head[0, n]
        found = slot >= 0.0
        head[0, count] = slot
        sources[count] = OVER + n

        @pl.when(found)
        def _():
            places[slot.astype(jnp.int32)] = OVER + n

        return count + found.astype(jnp.int32)

    count = lax.fori_loop(0, CAP, take_edge, count)
    for copy in bulk:
        copy.wait()

    def take_far(n, count):
        slot = far_head[0, n]
        found = slot >= 0.0
        place = places[jnp.maximum(slot.astype(jnp.int32), 0)]
        head[0, count] = slot
        sources[count] = OVER + CAP + n

        @pl.when(found & (place >= 0))
        def _():
            blocks[block(place), :] = blocks[block(place), :] + blocks[block(OVER + CAP + n), :]

        return count + (found & (place < 0)).astype(jnp.int32)

    count = lax.fori_loop(0, CAP, take_far, count)

    def blank(n, _):
        head[0, n] = -1.0
        return 0

    lax.fori_loop(count, SLOTS + OVER, blank, 0)
    left = jnp.maximum(count - FIXED, 0)
    tail_count[0] = left
    head[1, 0] = left.astype(F32)
    label = pltpu.make_async_copy(head, first_out.at[pl.ds(0, HEAD)], in_sems.at[0])
    label.start()

    def send_first(n, _):
        pltpu.make_async_copy(blocks.at[block(sources[n])], first_out.at[payload_block(n)], out_sems.at[n]).start()
        return 0

    def send_second(n, _):
        pltpu.make_async_copy(blocks.at[block(sources[n])], second_out.at[block(n - PART)], out_sems.at[n]).start()
        return 0

    lax.fori_loop(0, jnp.minimum(count, PART), send_first, 0)
    lax.fori_loop(PART, jnp.minimum(count, FIXED), send_second, 0)

    def send_tail(n, _):
        for k, (size, out) in enumerate(zip(TAILS, tail_outs)):

            @pl.when(left <= size)
            def _():
                source = blocks.at[block(sources[FIXED + n])]
                pltpu.make_async_copy(source, out.at[block(n)], tail_sems.at[k, n]).start()

        return 0

    lax.fori_loop(0, left, send_tail, 0)

    def drain(n, _):
        pltpu.make_async_copy(blocks.at[block(0)], second_out.at[block(0)], out_sems.at[n]).wait()
        return 0

    lax.fori_loop(0, jnp.minimum(count, FIXED), drain, 0)

    def drain_tail(n, _):
        for k, size in enumerate(TAILS):

            @pl.when(left <= size)
            def _():
                pltpu.make_async_copy(blocks.at[block(0)], second_out.at[block(0)], tail_sems.at[k, n]).wait()

        return 0

    lax.fori_loop(0, left, drain_tail, 0)
    label.wait()


def merge(over, edge, far):
    return pl.pallas_call(
        merge_kernel,
        out_shape=(
            payload_type(PART),
            jax.ShapeDtypeStruct((SECOND * SK, SK), F32),
            *[jax.ShapeDtypeStruct((size * SK, SK), F32) for size in TAILS],
            jax.ShapeDtypeStruct((1,), jnp.int32),
        ),
        in_specs=[ANY] * 3,
        out_specs=(ANY,) * (2 + len(TAILS)) + (SMEM,),
        scratch_shapes=[
            pltpu.VMEM(((OVER + 2 * CAP) * SK, SK), F32),
            pltpu.SMEM((HEAD, 128), F32),
            pltpu.SMEM((HEAD, 128), F32),
            pltpu.SMEM((HEAD, 128), F32),
            pltpu.SMEM((SLOTS,), jnp.int32),
            pltpu.SMEM((SLOTS + OVER + 1,), jnp.int32),
            pltpu.SemaphoreType.DMA((5,)),
            pltpu.SemaphoreType.DMA((FIXED,)),
            pltpu.SemaphoreType.DMA((len(TAILS), TAILS[-1])),
        ],
        compiler_params=pltpu.CompilerParams(vmem_limit_bytes=VMEM_BYTES),
        cost_estimate=cost(1),
        name="merge",
    )(over, edge, far)


def settle_kernel(total_h, *refs):
    count = len(PARCELS)
    payloads, out, total = refs[:count], refs[count], refs[count + 1]
    blocks, heads, sems = refs[count + 2:2 * count + 2], refs[2 * count + 2:3 * count + 2], refs[-1]
    loads = [pltpu.make_async_copy(total_h, total, sems.at[0])]
    for n in range(count):
        loads.append(pltpu.make_async_copy(payloads[n].at[pl.ds(0, HEAD)], heads[n], sems.at[2 * n + 1]))
        size = PARCELS[n][0] * SK
        loads.append(pltpu.make_async_copy(payloads[n].at[pl.ds(HEAD, size)], blocks[n], sems.at[2 * n + 2]))
    for copy in loads:
        copy.start()
    loads[0].wait()
    for n, (size, base) in enumerate(PARCELS):
        loads[2 * n + 1].wait()
        loads[2 * n + 2].wait()

        def add(k, _):
            slot = heads[n][0, k].astype(jnp.int32) - base

            @pl.when((slot >= 0) & (slot < SLOTS))
            def _():
                total[slot] = total[slot] + blocks[n][block(k), :]

            return 0

        lax.fori_loop(0, size, add, 0)
    copy = pltpu.make_async_copy(total, out, sems.at[0])
    copy.start()
    copy.wait()


def settle(total, *payloads):
    return pl.pallas_call(
        settle_kernel,
        out_shape=block_type(SLOTS),
        in_specs=[ANY] * (1 + len(PARCELS)),
        out_specs=ANY,
        scratch_shapes=[
            pltpu.VMEM((SLOTS, SK, SK), F32),
            *[pltpu.VMEM((size * SK, SK), F32) for size, _ in PARCELS],
            *[pltpu.SMEM((HEAD, 128), F32) for _ in PARCELS],
            pltpu.SemaphoreType.DMA((1 + 2 * len(PARCELS),)),
        ],
        input_output_aliases={0: 0},
        compiler_params=pltpu.CompilerParams(vmem_limit_bytes=VMEM_BYTES),
        cost_estimate=cost(1),
        name="settle",
    )(total, *payloads)


def decide_kernel(own_count, first_h, near_h, partner_h, total_h, forward_out, branch, held, head, sems):
    names = pltpu.make_async_copy(first_h.at[pl.ds(0, HEAD)], head, sems.at[0])
    part = pltpu.make_async_copy(first_h.at[pl.ds(0, HEAD + OVER * SK)], held, sems.at[1])
    names.start()
    part.start()
    names.wait()
    left = jnp.maximum(own_count[0], head[1, 0].astype(jnp.int32))
    which = jnp.int32(0)
    for size in (0, *TAILS[:-1]):
        which = which + (left > size).astype(jnp.int32)
    branch[0] = which
    part.wait()
    copy = pltpu.make_async_copy(held, forward_out, sems.at[0])
    copy.start()
    copy.wait()


def decide(own_count, first, near, partner, total):
    return pl.pallas_call(
        decide_kernel,
        out_shape=(payload_type(OVER), jax.ShapeDtypeStruct((1,), jnp.int32)),
        in_specs=[SMEM, ANY, ANY, ANY, ANY],
        out_specs=(ANY, SMEM),
        scratch_shapes=[
            pltpu.VMEM((HEAD + OVER * SK, SK), F32),
            pltpu.SMEM((HEAD, 128), F32),
            pltpu.SemaphoreType.DMA((2,)),
        ],
        compiler_params=pltpu.CompilerParams(vmem_limit_bytes=VMEM_BYTES),
        cost_estimate=cost(1),
        name="decide",
    )(own_count, first, near, partner, total)


def add_late_kernel(begin, total_h, first_h, blocks_h, out, total, blocks, head, sems, slot_sems):
    count = total.shape[0]
    names = pltpu.make_async_copy(first_h.at[pl.ds(0, HEAD)], head, sems.at[0])
    bulk = pltpu.make_async_copy(blocks_h, blocks, sems.at[1])
    names.start()
    bulk.start()
    names.wait()

    def each(act):
        def step(n, _):
            slot = head[0, begin + n].astype(jnp.int32)

            @pl.when((slot >= 0) & (slot < SLOTS))
            def _():
                act(n, slot)

            return 0

        lax.fori_loop(0, count, step, 0)

    def load(n, slot):
        pltpu.make_async_copy(total_h.at[slot], total.at[n], slot_sems.at[0, n]).start()

    def add(n, slot):
        pltpu.make_async_copy(total_h.at[slot], total.at[n], slot_sems.at[0, n]).wait()
        total[n] = total[n] + blocks[block(n), :]
        pltpu.make_async_copy(total.at[n], out.at[slot], slot_sems.at[1, n]).start()

    def drain(n, slot):
        pltpu.make_async_copy(total.at[n], out.at[slot], slot_sems.at[1, n]).wait()

    each(load)
    bulk.wait()
    each(add)
    each(drain)


def add_late(total, first, blocks, begin):
    count = blocks.shape[0] // SK
    return pl.pallas_call(
        functools.partial(add_late_kernel, begin),
        out_shape=block_type(SLOTS),
        in_specs=[ANY] * 3,
        out_specs=ANY,
        scratch_shapes=[
            pltpu.VMEM((count, SK, SK), F32),
            pltpu.VMEM((count * SK, SK), F32),
            pltpu.SMEM((HEAD, 128), F32),
            pltpu.SemaphoreType.DMA((2,)),
            pltpu.SemaphoreType.DMA((2, count)),
        ],
        input_output_aliases={0: 0},
        compiler_params=pltpu.CompilerParams(vmem_limit_bytes=VMEM_BYTES),
        cost_estimate=cost(1),
        name="add_late",
    )(total, first, blocks)


def place_kernel(coarse, received, out, held, sems):
    parity = lax.rem(lax.axis_index("box"), 2)
    copy = pltpu.make_async_copy(received, held, sems.at[0])
    copy.start()
    copy.wait()
    copy = pltpu.make_async_copy(held, out.at[pl.ds(2 - 2 * parity, 2)], sems.at[1])
    copy.start()
    copy.wait()


def place(coarse, received):
    return pl.pallas_call(
        place_kernel,
        out_shape=jax.ShapeDtypeStruct(coarse.shape, F32),
        in_specs=[ANY, ANY],
        out_specs=ANY,
        scratch_shapes=[pltpu.VMEM((BOXES, NB // 2, SK, SK), F32), pltpu.SemaphoreType.DMA((2,))],
        input_output_aliases={0: 0},
        compiler_params=pltpu.CompilerParams(vmem_limit_bytes=VMEM_BYTES),
        cost_estimate=cost(1),
        name="place",
    )(coarse, received)


def moved(value, route):
    devices = lax.axis_size("box")
    return lax.ppermute(value, "box", [(i, route(i) % devices) for i in range(devices)])


def other_core(i):
    return i ^ 1


def across(i):
    return i + 1 if i % 2 else i - 1


def beyond(i):
    return i + 2 if i % 2 else i - 2


def body(self_block, interp, split, inverse_block, row_blocks, col_blocks, pairs, targets, pair_blocks):
    targets = jnp.transpose(targets, (0, 2, 1))
    pairs = jnp.transpose(pairs, (0, 2, 1))
    rows = row_blocks.reshape(BOXES, ROWS, P_SIZE)
    cols = col_blocks.reshape(BOXES, ROWS, P_SIZE)
    near, over, far, edge, partner = front(targets, pairs, split, interp, cols, rows, inverse_block)
    near = moved(near, beyond)
    far = moved(far, other_core)
    partner = moved(partner, other_core)
    first, second, *tails, own_count = merge(over, edge, far)
    total, coarse, skel = rest(targets, pairs, split, interp, cols, rows, inverse_block, self_block, pair_blocks)
    first = moved(first, across)
    second = moved(second, across)
    skel = moved(skel, other_core)
    coarse = place(coarse, skel)
    forward, branch = decide(own_count, first, near, partner, total)
    forward = moved(forward, other_core)

    def none(total, near, partner, first, forward, *tails):
        return settle(total, near, partner, first, forward)

    def some(which):
        def send(total, near, partner, first, forward, *tails):
            tail = moved(tails[which], across)
            total = settle(total, near, partner, first, forward)
            return add_late(total, first, tail, FIXED)

        return send

    branches = [none] + [some(n) for n in range(len(TAILS))]
    total = lax.switch(branch[0], branches, total, near, partner, first, forward, *tails)
    total = add_late(total, first, second, PART)
    return total, coarse[None]


def solution(mesh):
    return jax.shard_map(
        body,
        mesh=mesh,
        in_specs=(
            P("box", None, None),
            P("box", None, None),
            P("box", None),
            P("box", None, None),
            P("box", None, None, None),
            P("box", None, None, None),
            P("box", None, None),
            P("box", None, None),
            P("box", None, None),
        ),
        out_specs=(P("box", None, None), P("box", None, None, None, None)),
        check_vma=False,
    )
```

```python
import functools

import jax
import jax.numpy as jnp
from jax import lax
from jax.experimental import pallas as pl
from jax.experimental.pallas import tpu as pltpu
from jax.sharding import PartitionSpec as P

P_SIZE = 512
SK = 128
RD = 384
BOXES = 2
NB = 8
PAIRS = 24
SLOTS = 48
CAP = 32
ROWS = NB * SK
TILE = 512
NEAR = 20
OVER = CAP - NEAR
PART = 12
SECOND = 20
FIXED = PART + SECOND
TAILS = (3, 5, 7, 9, 12, 28)
MARK = 64
PARCELS = ((NEAR, 0), (CAP, 0), (PART, 0), (OVER, MARK))
HEAD = 8
VMEM_BYTES = 65_200_000
F32 = jnp.float32
BF16 = jnp.bfloat16
NT = (((1,), (1,)), ((), ()))

ANY = pl.BlockSpec(memory_space=pl.ANY)
SMEM = pl.BlockSpec(memory_space=pltpu.SMEM)


def block_type(count):
    return jax.ShapeDtypeStruct((count, SK, SK), F32)


def cost(us):
    return pl.CostEstimate(flops=us * 1_000_000_000, bytes_accessed=0, transcendentals=0)


def payload_type(count):
    return jax.ShapeDtypeStruct((HEAD + count * SK, SK), F32)


def input_copies(hbm, vmem, sems):
    out = []
    for box in range(BOXES):
        out.append([
            pltpu.make_async_copy(source.at[box], target.at[box], sems.at[box, n])
            for n, (source, target) in enumerate(zip(hbm, vmem))
        ])
    return out


def compressor_of(split, interp, box):
    points = lax.broadcasted_iota(jnp.int32, (P_SIZE, RD), 0)
    pick_red = points == split[box:box + 1, :RD]
    points = lax.broadcasted_iota(jnp.int32, (P_SIZE, SK), 0)
    pick_skel = (points == split[box:box + 1, RD:]).astype(F32).astype(BF16)
    spread = lax.dot_general(pick_skel, interp[box], NT, preferred_element_type=F32)
    return (jnp.where(pick_red, 1.0, 0.0) - spread).astype(BF16), pick_skel


def mul(a, b):
    return jnp.dot(a, b, preferred_element_type=F32)


def products(box, copies, split, interp, inverse, rows, cols, w_far, y_near, compressor, grams):
    copies[0].wait()
    comp, pick_skel = compressor_of(split, interp, box)
    compressor[...] = comp
    copies[1].wait()

    def far(n, _):
        at = pl.ds(pl.multiple_of(n * TILE, TILE), TILE)
        w_far[at, :] = mul(cols[box, at, :], compressor[...]).astype(BF16)
        return 0

    lax.fori_loop(0, ROWS // TILE, far, 0, unroll=True)
    copies[2].wait()
    copies[3].wait()

    def near(n, _):
        at = pl.ds(pl.multiple_of(n * TILE, TILE), TILE)
        x_near = mul(rows[box, at, :], compressor[...]).astype(BF16)
        y_near[at, :] = mul(x_near, inverse[box]).astype(BF16)
        return 0

    lax.fori_loop(0, ROWS // TILE, near, 0, unroll=True)

    def gram(n, _):
        at = pl.ds(pl.multiple_of(n * TILE, TILE), TILE)
        tile = lax.dot_general(y_near[...], w_far[at, :], NT, preferred_element_type=F32)
        for i in range(NB):
            for k in range(TILE // SK):
                grams[i, n * (TILE // SK) + k] = tile[i * SK:(i + 1) * SK, k * SK:(k + 1) * SK]
        return 0

    lax.fori_loop(0, ROWS // TILE, gram, 0, unroll=True)
    return pick_skel


def block(n):
    return pl.ds(pl.multiple_of(n * SK, SK), SK)


def payload_block(n):
    return pl.ds(pl.multiple_of(HEAD + n * SK, 8), SK)


def work_list(targets, pairs, todo, used, places, first_touch):
    device = lax.axis_index("box")
    odd = lax.rem(device, 2) == 1
    all_slots = lax.axis_size("box") * SLOTS
    here = device * SLOTS
    ends = []
    for box in range(BOXES):

        def enter(pair, end):
            numbers = [pairs[box, 0, pair], pairs[box, 1, pair]]
            for side in range(2):
                away = targets[box, side, pair] - here
                away = jnp.where(away >= all_slots // 2, away - all_slots, away)
                away = jnp.where(away < -(all_slots // 2), away + all_slots, away)
                hops = jnp.int32(-2)
                for low in range(-1, 3):
                    hops = hops + (away >= low * SLOTS).astype(jnp.int32)
                slot = away - hops * SLOTS
                hops = jnp.where(odd, hops, -hops)
                place = jnp.int32(len(places) * SLOTS)
                for n, want in enumerate(places):
                    place = jnp.where(hops == want, slot + n * SLOTS, place)
                entry = place * 128 + numbers[side] * 16 + numbers[1 - side] * 2
                if first_touch:
                    entry = entry + used[place]
                    used[place] = 1
                todo[box, end] = entry
                end = end + (place < len(places) * SLOTS).astype(jnp.int32)
            return end

        ends.append(lax.fori_loop(0, PAIRS, enter, jnp.int32(0), unroll=2))
    return ends


def listed(entry):
    return lax.shift_right_logical(entry, 7), lax.shift_right_logical(entry, 4) & 7, lax.shift_right_logical(entry, 1) & 7


def front_kernel(targets_h, pairs_h, split_h, interp_h, cols_h, rows_h, inverse_h,
                 near_out, over_out, far_out, edge_out, partner_out,
                 interp, cols, rows, inverse, w_far, y_near, compressor, grams, split, acc, targets, pairs, todo, used,
                 near_head, far_head, edge_head, partner_head, in_sems, out_sems, small_sems):
    small = [
        pltpu.make_async_copy(targets_h, targets, small_sems.at[0]),
        pltpu.make_async_copy(pairs_h, pairs, small_sems.at[1]),
        pltpu.make_async_copy(split_h, split, small_sems.at[2]),
    ]
    for copy in small:
        copy.start()
    copies = input_copies((interp_h, cols_h, rows_h, inverse_h), (interp, cols, rows, inverse), in_sems)
    for box in range(BOXES):
        for copy in copies[box]:
            copy.start()

    def clear_used(n, _):
        used[n] = 0
        return 0

    lax.fori_loop(0, 4 * SLOTS, clear_used, 0, unroll=8)
    for copy in small:
        copy.wait()
    ends = work_list(targets, pairs, todo, used, (2, -2, 1, -1), True)

    def number(n, counts):
        name = n.astype(F32)
        near_head[0, counts[0]] = name
        edge_head[1, counts[0]] = name
        far_head[0, counts[1]] = name
        edge_head[0, counts[2]] = name
        partner_head[0, counts[3]] = name
        return tuple(count + used[base * SLOTS + n] for base, count in enumerate(counts))

    counts = lax.fori_loop(0, SLOTS, number, (jnp.int32(0),) * 4, unroll=4)
    rows_of = (near_head.at[0], far_head.at[0], edge_head.at[0], partner_head.at[0], edge_head.at[1])
    for row, count in zip(rows_of, (*counts, counts[0])):

        def blank(n, _):
            row[n] = -1.0
            return 0

        lax.fori_loop(count, CAP, blank, 0)

    for box in range(BOXES):
        products(box, copies[box], split, interp, inverse, rows, cols, w_far, y_near, compressor, grams)

        def add(n, _):
            entry = todo[box, n]
            place, i, j = listed(entry)
            acc[place] = jnp.where((entry & 1) == 1, acc[place], 0.0) - grams[i, j]
            return 0

        lax.fori_loop(0, ends[box], add, 0)

    labels = [
        pltpu.make_async_copy(near_head, near_out.at[pl.ds(0, HEAD)], small_sems.at[0]),
        pltpu.make_async_copy(far_head, far_out.at[pl.ds(0, HEAD)], small_sems.at[1]),
        pltpu.make_async_copy(edge_head, edge_out.at[pl.ds(0, HEAD)], small_sems.at[2]),
        pltpu.make_async_copy(partner_head, partner_out.at[pl.ds(0, HEAD)], small_sems.at[3]),
    ]
    for copy in labels:
        copy.start()
    near_count = jnp.minimum(counts[0], NEAR)
    lots = (
        (0, near_head, near_out, 0, near_count),
        (0, near_head, over_out, NEAR, counts[0]),
        (1, far_head, far_out, 0, counts[1]),
        (2, edge_head, edge_out, 0, counts[2]),
        (3, partner_head, partner_out, 0, counts[3]),
    )
    for base, head, out, begin, end in lots:

        def send(n, _):
            source = acc.at[base * SLOTS + head[0, n].astype(jnp.int32)]
            rows_at = block(n - begin) if begin else payload_block(n)
            pltpu.make_async_copy(source, out.at[rows_at], out_sems.at[base, n]).start()
            return 0

        lax.fori_loop(begin, end, send, 0)
    for base in range(4):

        def drain(n, _):
            pltpu.make_async_copy(acc.at[base], far_out.at[payload_block(0)], out_sems.at[base, n]).wait()
            return 0

        lax.fori_loop(0, counts[base], drain, 0)
    for copy in labels:
        copy.wait()


def box_scratch():
    return [
        pltpu.VMEM((BOXES, RD, SK), BF16),
        pltpu.VMEM((BOXES, ROWS, P_SIZE), BF16),
        pltpu.VMEM((BOXES, ROWS, P_SIZE), BF16),
        pltpu.VMEM((BOXES, RD, RD), BF16),
        pltpu.VMEM((ROWS, RD), BF16),
        pltpu.VMEM((ROWS, RD), BF16),
        pltpu.VMEM((P_SIZE, RD), BF16),
        pltpu.VMEM((NB, NB, SK, SK), F32),
    ]


def front(targets, pairs, split, interp, cols, rows, inverse):
    return pl.pallas_call(
        front_kernel,
        out_shape=(
            payload_type(NEAR), jax.ShapeDtypeStruct((OVER * SK, SK), F32),
            payload_type(CAP), payload_type(CAP), payload_type(CAP),
        ),
        in_specs=[ANY] * 7,
        out_specs=(ANY,) * 5,
        scratch_shapes=box_scratch() + [
            pltpu.VMEM((BOXES, P_SIZE), jnp.int32),
            pltpu.VMEM((4 * SLOTS + 1, SK, SK), F32),
            pltpu.SMEM((BOXES, 2, PAIRS), jnp.int32),
            pltpu.SMEM((BOXES, 2, PAIRS), jnp.int32),
            pltpu.SMEM((BOXES, 2 * PAIRS + 1), jnp.int32),
            pltpu.SMEM((4 * SLOTS + 1,), jnp.int32),
            pltpu.SMEM((HEAD, 128), F32),
            pltpu.SMEM((HEAD, 128), F32),
            pltpu.SMEM((HEAD, 128), F32),
            pltpu.SMEM((HEAD, 128), F32),
            pltpu.SemaphoreType.DMA((BOXES, 4)),
            pltpu.SemaphoreType.DMA((4, CAP)),
            pltpu.SemaphoreType.DMA((4,)),
        ],
        compiler_params=pltpu.CompilerParams(vmem_limit_bytes=VMEM_BYTES),
        cost_estimate=cost(1),
        name="front",
    )(targets, pairs, split, interp, cols, rows, inverse)


def rest_kernel(targets_h, pairs_h, split_h, interp_h, cols_h, rows_h, inverse_h, self_h, start_h,
                total_out, coarse_out, skel_out,
                interp, cols, rows, inverse, self_block, w_far, y_near, compressor, grams, split, start, acc, skel,
                targets, pairs, todo, in_sems, out_sems, small_sems):
    small = [
        pltpu.make_async_copy(targets_h, targets, small_sems.at[0]),
        pltpu.make_async_copy(pairs_h, pairs, small_sems.at[1]),
        pltpu.make_async_copy(split_h, split, small_sems.at[2]),
    ]
    for copy in small:
        copy.start()
    copies = input_copies((interp_h, cols_h, rows_h, inverse_h, self_h), (interp, cols, rows, inverse, self_block), in_sems)
    start_copy = pltpu.make_async_copy(start_h, start, out_sems.at[4])
    for copy in copies[0]:
        copy.start()
    start_copy.start()
    for copy in copies[1]:
        copy.start()

    for copy in small:
        copy.wait()
    ends = work_list(targets, pairs, todo, None, (0,), False)
    start_copy.wait()

    def widen(n, _):
        acc[n] = start[n].astype(F32)
        return 0

    lax.fori_loop(0, SLOTS, widen, 0)
    parity = lax.rem(lax.axis_index("box"), 2)
    for box in range(BOXES):
        pick_skel = products(box, copies[box], split, interp, inverse, rows, cols, w_far, y_near, compressor, grams)

        def add(n, _):
            place, i, j = listed(todo[box, n])
            acc[place] = acc[place] - grams[i, j]
            return 0

        lax.fori_loop(0, ends[box], add, 0)
        copies[box][4].wait()
        x_self = mul(self_block[box], compressor[...]).astype(BF16)
        y_self = mul(x_self, inverse[box]).astype(BF16)
        pick_rows = pick_skel.astype(F32).T.astype(BF16)
        for n in range(ROWS // TILE):
            at = slice(n * TILE, (n + 1) * TILE)
            base = lax.dot_general(pick_rows, cols[box, at, :], NT, preferred_element_type=F32)
            base = base - lax.dot_general(y_self, w_far[at, :], NT, preferred_element_type=F32)
            for k in range(TILE // SK):
                j = n * (TILE // SK) + k
                skel[j // 4, box, j % 4] = base[:, k * SK:(k + 1) * SK]

    outs = [
        pltpu.make_async_copy(acc, total_out, out_sems.at[1]),
        pltpu.make_async_copy(skel.at[parity], coarse_out.at[pl.ds(2 * parity, 2)], out_sems.at[2]),
        pltpu.make_async_copy(skel.at[1 - parity], skel_out, out_sems.at[3]),
    ]
    for copy in outs:
        copy.start()
    for copy in outs:
        copy.wait()


def rest(targets, pairs, split, interp, cols, rows, inverse, self_block, start):
    scratch = box_scratch()
    scratch.insert(4, pltpu.VMEM((BOXES, SK, P_SIZE), BF16))
    return pl.pallas_call(
        rest_kernel,
        out_shape=(
            block_type(SLOTS),
            jax.ShapeDtypeStruct((2 * BOXES, NB // 2, SK, SK), F32),
            jax.ShapeDtypeStruct((BOXES, NB // 2, SK, SK), F32),
        ),
        in_specs=[ANY] * 9,
        out_specs=(ANY,) * 3,
        scratch_shapes=scratch + [
            pltpu.VMEM((BOXES, P_SIZE), jnp.int32),
            pltpu.VMEM((SLOTS, SK, SK), BF16),
            pltpu.VMEM((SLOTS, SK, SK), F32),
            pltpu.VMEM((2, BOXES, NB // 2, SK, SK), F32),
            pltpu.SMEM((BOXES, 2, PAIRS), jnp.int32),
            pltpu.SMEM((BOXES, 2, PAIRS), jnp.int32),
            pltpu.SMEM((BOXES, 2 * PAIRS + 1), jnp.int32),
            pltpu.SemaphoreType.DMA((BOXES, 5)),
            pltpu.SemaphoreType.DMA((5,)),
            pltpu.SemaphoreType.DMA((3,)),
        ],
        compiler_params=pltpu.CompilerParams(vmem_limit_bytes=VMEM_BYTES),
        cost_estimate=cost(1),
        name="rest",
    )(targets, pairs, split, interp, cols, rows, inverse, self_block, start)


def merge_kernel(over_h, edge_h, far_h, first_out, second_out, *refs):
    tail_outs = refs[:len(TAILS)]
    tail_count, blocks, edge_head, far_head, head, places, sources, in_sems, out_sems, tail_sems = refs[len(TAILS):]
    heads = [
        pltpu.make_async_copy(edge_h.at[pl.ds(0, HEAD)], edge_head, in_sems.at[0]),
        pltpu.make_async_copy(far_h.at[pl.ds(0, HEAD)], far_head, in_sems.at[1]),
    ]
    bulk = [
        pltpu.make_async_copy(over_h, blocks.at[pl.ds(0, OVER * SK)], in_sems.at[2]),
        pltpu.make_async_copy(edge_h.at[pl.ds(HEAD, CAP * SK)], blocks.at[pl.ds(OVER * SK, CAP * SK)], in_sems.at[3]),
        pltpu.make_async_copy(far_h.at[pl.ds(HEAD, CAP * SK)], blocks.at[pl.ds((OVER + CAP) * SK, CAP * SK)], in_sems.at[4]),
    ]
    for copy in heads + bulk:
        copy.start()

    def clear(n, _):
        places[n] = -1
        return 0

    lax.fori_loop(0, SLOTS, clear, 0, unroll=8)
    for copy in heads:
        copy.wait()

    def take_over(n, count):
        slot = edge_head[1, NEAR + n]
        head[0, count] = slot + MARK
        sources[count] = n
        return count + (slot >= 0.0).astype(jnp.int32)

    count = lax.fori_loop(0, OVER, take_over, jnp.int32(0))

    def take_edge(n, count):
        slot = edge_head[0, n]
        found = slot >= 0.0
        head[0, count] = slot
        sources[count] = OVER + n

        @pl.when(found)
        def _():
            places[slot.astype(jnp.int32)] = OVER + n

        return count + found.astype(jnp.int32)

    count = lax.fori_loop(0, CAP, take_edge, count)
    for copy in bulk:
        copy.wait()

    def take_far(n, count):
        slot = far_head[0, n]
        found = slot >= 0.0
        place = places[jnp.maximum(slot.astype(jnp.int32), 0)]
        head[0, count] = slot
        sources[count] = OVER + CAP + n

        @pl.when(found & (place >= 0))
        def _():
            blocks[block(place), :] = blocks[block(place), :] + blocks[block(OVER + CAP + n), :]

        return count + (found & (place < 0)).astype(jnp.int32)

    count = lax.fori_loop(0, CAP, take_far, count)

    def blank(n, _):
        head[0, n] = -1.0
        return 0

    lax.fori_loop(count, SLOTS + OVER, blank, 0)
    left = jnp.maximum(count - FIXED, 0)
    tail_count[0] = left
    head[1, 0] = left.astype(F32)
    label = pltpu.make_async_copy(head, first_out.at[pl.ds(0, HEAD)], in_sems.at[0])
    label.start()

    def send_first(n, _):
        pltpu.make_async_copy(blocks.at[block(sources[n])], first_out.at[payload_block(n)], out_sems.at[n]).start()
        return 0

    def send_second(n, _):
        pltpu.make_async_copy(blocks.at[block(sources[n])], second_out.at[block(n - PART)], out_sems.at[n]).start()
        return 0

    lax.fori_loop(0, jnp.minimum(count, PART), send_first, 0)
    lax.fori_loop(PART, jnp.minimum(count, FIXED), send_second, 0)

    def send_tail(n, _):
        for k, (size, out) in enumerate(zip(TAILS, tail_outs)):

            @pl.when(left <= size)
            def _():
                source = blocks.at[block(sources[FIXED + n])]
                pltpu.make_async_copy(source, out.at[block(n)], tail_sems.at[k, n]).start()

        return 0

    lax.fori_loop(0, left, send_tail, 0)

    def drain(n, _):
        pltpu.make_async_copy(blocks.at[block(0)], second_out.at[block(0)], out_sems.at[n]).wait()
        return 0

    lax.fori_loop(0, jnp.minimum(count, FIXED), drain, 0)

    def drain_tail(n, _):
        for k, size in enumerate(TAILS):

            @pl.when(left <= size)
            def _():
                pltpu.make_async_copy(blocks.at[block(0)], second_out.at[block(0)], tail_sems.at[k, n]).wait()

        return 0

    lax.fori_loop(0, left, drain_tail, 0)
    label.wait()


def merge(over, edge, far):
    return pl.pallas_call(
        merge_kernel,
        out_shape=(
            payload_type(PART),
            jax.ShapeDtypeStruct((SECOND * SK, SK), F32),
            *[jax.ShapeDtypeStruct((size * SK, SK), F32) for size in TAILS],
            jax.ShapeDtypeStruct((1,), jnp.int32),
        ),
        in_specs=[ANY] * 3,
        out_specs=(ANY,) * (2 + len(TAILS)) + (SMEM,),
        scratch_shapes=[
            pltpu.VMEM(((OVER + 2 * CAP) * SK, SK), F32),
            pltpu.SMEM((HEAD, 128), F32),
            pltpu.SMEM((HEAD, 128), F32),
            pltpu.SMEM((HEAD, 128), F32),
            pltpu.SMEM((SLOTS,), jnp.int32),
            pltpu.SMEM((SLOTS + OVER + 1,), jnp.int32),
            pltpu.SemaphoreType.DMA((5,)),
            pltpu.SemaphoreType.DMA((FIXED,)),
            pltpu.SemaphoreType.DMA((len(TAILS), TAILS[-1])),
        ],
        compiler_params=pltpu.CompilerParams(vmem_limit_bytes=VMEM_BYTES),
        cost_estimate=cost(1),
        name="merge",
    )(over, edge, far)


def settle_kernel(total_h, *refs):
    count = len(PARCELS)
    payloads, out, total = refs[:count], refs[count], refs[count + 1]
    blocks, heads, sems = refs[count + 2:2 * count + 2], refs[2 * count + 2:3 * count + 2], refs[-1]
    loads = [pltpu.make_async_copy(total_h, total, sems.at[0])]
    for n in range(count):
        loads.append(pltpu.make_async_copy(payloads[n].at[pl.ds(0, HEAD)], heads[n], sems.at[2 * n + 1]))
        size = PARCELS[n][0] * SK
        loads.append(pltpu.make_async_copy(payloads[n].at[pl.ds(HEAD, size)], blocks[n], sems.at[2 * n + 2]))
    for copy in loads:
        copy.start()
    loads[0].wait()
    for n, (size, base) in enumerate(PARCELS):
        loads[2 * n + 1].wait()
        loads[2 * n + 2].wait()

        def add(k, _):
            slot = heads[n][0, k].astype(jnp.int32) - base

            @pl.when((slot >= 0) & (slot < SLOTS))
            def _():
                total[slot] = total[slot] + blocks[n][block(k), :]

            return 0

        lax.fori_loop(0, size, add, 0)
    copy = pltpu.make_async_copy(total, out, sems.at[0])
    copy.start()
    copy.wait()


def settle(total, *payloads):
    return pl.pallas_call(
        settle_kernel,
        out_shape=block_type(SLOTS),
        in_specs=[ANY] * (1 + len(PARCELS)),
        out_specs=ANY,
        scratch_shapes=[
            pltpu.VMEM((SLOTS, SK, SK), F32),
            *[pltpu.VMEM((size * SK, SK), F32) for size, _ in PARCELS],
            *[pltpu.SMEM((HEAD, 128), F32) for _ in PARCELS],
            pltpu.SemaphoreType.DMA((1 + 2 * len(PARCELS),)),
        ],
        input_output_aliases={0: 0},
        compiler_params=pltpu.CompilerParams(vmem_limit_bytes=VMEM_BYTES),
        cost_estimate=cost(1),
        name="settle",
    )(total, *payloads)


def decide_kernel(own_count, first_h, near_h, partner_h, total_h, forward_out, branch, held, head, sems):
    names = pltpu.make_async_copy(first_h.at[pl.ds(0, HEAD)], head, sems.at[0])
    part = pltpu.make_async_copy(first_h.at[pl.ds(0, HEAD + OVER * SK)], held, sems.at[1])
    names.start()
    part.start()
    names.wait()
    left = jnp.maximum(own_count[0], head[1, 0].astype(jnp.int32))
    which = jnp.int32(0)
    for size in (0, *TAILS[:-1]):
        which = which + (left > size).astype(jnp.int32)
    branch[0] = which
    part.wait()
    copy = pltpu.make_async_copy(held, forward_out, sems.at[0])
    copy.start()
    copy.wait()


def decide(own_count, first, near, partner, total):
    return pl.pallas_call(
        decide_kernel,
        out_shape=(payload_type(OVER), jax.ShapeDtypeStruct((1,), jnp.int32)),
        in_specs=[SMEM, ANY, ANY, ANY, ANY],
        out_specs=(ANY, SMEM),
        scratch_shapes=[
            pltpu.VMEM((HEAD + OVER * SK, SK), F32),
            pltpu.SMEM((HEAD, 128), F32),
            pltpu.SemaphoreType.DMA((2,)),
        ],
        compiler_params=pltpu.CompilerParams(vmem_limit_bytes=VMEM_BYTES),
        cost_estimate=cost(1),
        name="decide",
    )(own_count, first, near, partner, total)


def finish_kernel(begin, total_h, first_h, blocks_h, coarse_h, received, out, coarse_out,
                  total, blocks, head, sems, slot_sems, held, held_sems):
    other = lax.rem(lax.axis_index("box") + 1, 2)
    arrive = pltpu.make_async_copy(received, held, held_sems.at[0])
    arrive.start()

    def hand_over():
        arrive.wait()
        pltpu.make_async_copy(held, coarse_out.at[pl.ds(2 * other, 2)], held_sems.at[1]).start()

    add_late_kernel(begin, total_h, first_h, blocks_h, out, total, blocks, head, sems, slot_sems, hand_over)
    pltpu.make_async_copy(held, coarse_out.at[pl.ds(2 * other, 2)], held_sems.at[1]).wait()


def add_late_kernel(begin, total_h, first_h, blocks_h, out, total, blocks, head, sems, slot_sems, meanwhile=None):
    count = total.shape[0]
    names = pltpu.make_async_copy(first_h.at[pl.ds(0, HEAD)], head, sems.at[0])
    bulk = pltpu.make_async_copy(blocks_h, blocks, sems.at[1])
    names.start()
    bulk.start()
    names.wait()

    def each(act):
        def step(n, _):
            slot = head[0, begin + n].astype(jnp.int32)

            @pl.when((slot >= 0) & (slot < SLOTS))
            def _():
                act(n, slot)

            return 0

        lax.fori_loop(0, count, step, 0)

    def load(n, slot):
        pltpu.make_async_copy(total_h.at[slot], total.at[n], slot_sems.at[0, n]).start()

    def add(n, slot):
        pltpu.make_async_copy(total_h.at[slot], total.at[n], slot_sems.at[0, n]).wait()
        total[n] = total[n] + blocks[block(n), :]
        pltpu.make_async_copy(total.at[n], out.at[slot], slot_sems.at[1, n]).start()

    def drain(n, slot):
        pltpu.make_async_copy(total.at[n], out.at[slot], slot_sems.at[1, n]).wait()

    each(load)
    if meanwhile is not None:
        meanwhile()
    bulk.wait()
    each(add)
    each(drain)


def add_late(total, first, blocks, begin):
    count = blocks.shape[0] // SK
    return pl.pallas_call(
        functools.partial(add_late_kernel, begin),
        out_shape=block_type(SLOTS),
        in_specs=[ANY] * 3,
        out_specs=ANY,
        scratch_shapes=[
            pltpu.VMEM((count, SK, SK), F32),
            pltpu.VMEM((count * SK, SK), F32),
            pltpu.SMEM((HEAD, 128), F32),
            pltpu.SemaphoreType.DMA((2,)),
            pltpu.SemaphoreType.DMA((2, count)),
        ],
        input_output_aliases={0: 0},
        compiler_params=pltpu.CompilerParams(vmem_limit_bytes=VMEM_BYTES),
        cost_estimate=cost(1),
        name="add_late",
    )(total, first, blocks)


def finish(total, first, blocks, begin, coarse, received):
    count = blocks.shape[0] // SK
    return pl.pallas_call(
        functools.partial(finish_kernel, begin),
        out_shape=(block_type(SLOTS), jax.ShapeDtypeStruct(coarse.shape, F32)),
        in_specs=[ANY] * 5,
        out_specs=(ANY, ANY),
        scratch_shapes=[
            pltpu.VMEM((count, SK, SK), F32),
            pltpu.VMEM((count * SK, SK), F32),
            pltpu.SMEM((HEAD, 128), F32),
            pltpu.SemaphoreType.DMA((2,)),
            pltpu.SemaphoreType.DMA((2, count)),
            pltpu.VMEM(received.shape, F32),
            pltpu.SemaphoreType.DMA((2,)),
        ],
        input_output_aliases={0: 0, 3: 1},
        compiler_params=pltpu.CompilerParams(vmem_limit_bytes=VMEM_BYTES),
        cost_estimate=cost(1),
        name="finish",
    )(total, first, blocks, coarse, received)


def moved(value, route):
    devices = lax.axis_size("box")
    return lax.ppermute(value, "box", [(i, route(i) % devices) for i in range(devices)])


def other_core(i):
    return i ^ 1


def across(i):
    return i + 1 if i % 2 else i - 1


def beyond(i):
    return i + 2 if i % 2 else i - 2


def body(self_block, interp, split, inverse_block, row_blocks, col_blocks, pairs, targets, pair_blocks):
    targets = jnp.transpose(targets, (0, 2, 1))
    pairs = jnp.transpose(pairs, (0, 2, 1))
    rows = row_blocks.reshape(BOXES, ROWS, P_SIZE)
    cols = col_blocks.reshape(BOXES, ROWS, P_SIZE)
    near, over, far, edge, partner = front(targets, pairs, split, interp, cols, rows, inverse_block)
    near = moved(near, beyond)
    far = moved(far, other_core)
    partner = moved(partner, other_core)
    first, second, *tails, own_count = merge(over, edge, far)
    total, coarse, skel = rest(targets, pairs, split, interp, cols, rows, inverse_block, self_block, pair_blocks)
    first = moved(first, across)
    second = moved(second, across)
    skel = moved(skel, other_core)
    forward, branch = decide(own_count, first, near, partner, total)
    forward = moved(forward, other_core)

    def none(total, near, partner, first, forward, *tails):
        return settle(total, near, partner, first, forward)

    def some(which):
        def send(total, near, partner, first, forward, *tails):
            tail = moved(tails[which], across)
            total = settle(total, near, partner, first, forward)
            return add_late(total, first, tail, FIXED)

        return send

    branches = [none] + [some(n) for n in range(len(TAILS))]
    total = lax.switch(branch[0], branches, total, near, partner, first, forward, *tails)
    total, coarse = finish(total, first, second, PART, coarse, skel)
    return total, coarse[None]


def solution(mesh):
    return jax.shard_map(
        body,
        mesh=mesh,
        in_specs=(
            P("box", None, None),
            P("box", None, None),
            P("box", None),
            P("box", None, None),
            P("box", None, None, None),
            P("box", None, None, None),
            P("box", None, None),
            P("box", None, None),
            P("box", None, None),
        ),
        out_specs=(P("box", None, None), P("box", None, None, None, None)),
        check_vma=False,
    )
```

```python
import functools

import jax
import jax.numpy as jnp
from jax import lax
from jax.experimental import pallas as pl
from jax.experimental.pallas import tpu as pltpu
from jax.sharding import PartitionSpec as P

P_SIZE = 512
SK = 128
RD = 384
BOXES = 2
NB = 8
PAIRS = 24
SLOTS = 48
CAP = 32
ROWS = NB * SK
TILE = 512
NEAR = 20
OVER = CAP - NEAR
PART = 12
SECOND = 20
FIXED = PART + SECOND
TAILS = (3, 5, 7, 8, 9, 10, 12, 28)
MARK = 64
PARCELS = ((NEAR, 0), (CAP, 0), (PART, 0), (OVER, MARK))
HEAD = 8
VMEM_BYTES = 65_200_000
F32 = jnp.float32
BF16 = jnp.bfloat16
NT = (((1,), (1,)), ((), ()))

ANY = pl.BlockSpec(memory_space=pl.ANY)
SMEM = pl.BlockSpec(memory_space=pltpu.SMEM)


def block_type(count):
    return jax.ShapeDtypeStruct((count, SK, SK), F32)


def cost(us):
    return pl.CostEstimate(flops=us * 1_000_000_000, bytes_accessed=0, transcendentals=0)


def payload_type(count):
    return jax.ShapeDtypeStruct((HEAD + count * SK, SK), F32)


def input_copies(hbm, vmem, sems):
    out = []
    for box in range(BOXES):
        out.append([
            pltpu.make_async_copy(source.at[box], target.at[box], sems.at[box, n])
            for n, (source, target) in enumerate(zip(hbm, vmem))
        ])
    return out


def compressor_of(split, interp, box):
    points = lax.broadcasted_iota(jnp.int32, (P_SIZE, RD), 0)
    pick_red = points == split[box:box + 1, :RD]
    points = lax.broadcasted_iota(jnp.int32, (P_SIZE, SK), 0)
    pick_skel = (points == split[box:box + 1, RD:]).astype(F32).astype(BF16)
    spread = lax.dot_general(pick_skel, interp[box], NT, preferred_element_type=F32)
    return (jnp.where(pick_red, 1.0, 0.0) - spread).astype(BF16), pick_skel


def mul(a, b):
    return jnp.dot(a, b, preferred_element_type=F32)


def products(box, copies, split, interp, inverse, rows, cols, w_far, y_near, compressor, grams):
    copies[0].wait()
    comp, pick_skel = compressor_of(split, interp, box)
    compressor[...] = comp
    copies[1].wait()

    def far(n, _):
        at = pl.ds(pl.multiple_of(n * TILE, TILE), TILE)
        w_far[at, :] = mul(cols[box, at, :], compressor[...]).astype(BF16)
        return 0

    lax.fori_loop(0, ROWS // TILE, far, 0, unroll=True)
    copies[2].wait()
    copies[3].wait()

    def near(n, _):
        at = pl.ds(pl.multiple_of(n * TILE, TILE), TILE)
        x_near = mul(rows[box, at, :], compressor[...]).astype(BF16)
        y_near[at, :] = mul(x_near, inverse[box]).astype(BF16)
        return 0

    lax.fori_loop(0, ROWS // TILE, near, 0, unroll=True)

    def gram(n, _):
        at = pl.ds(pl.multiple_of(n * TILE, TILE), TILE)
        tile = lax.dot_general(y_near[...], w_far[at, :], NT, preferred_element_type=F32)
        for i in range(NB):
            for k in range(TILE // SK):
                grams[i, n * (TILE // SK) + k] = tile[i * SK:(i + 1) * SK, k * SK:(k + 1) * SK]
        return 0

    lax.fori_loop(0, ROWS // TILE, gram, 0, unroll=True)
    return pick_skel


def block(n):
    return pl.ds(pl.multiple_of(n * SK, SK), SK)


def payload_block(n):
    return pl.ds(pl.multiple_of(HEAD + n * SK, 8), SK)


def work_list(targets, pairs, todo, used, places, first_touch):
    device = lax.axis_index("box")
    odd = lax.rem(device, 2) == 1
    all_slots = lax.axis_size("box") * SLOTS
    here = device * SLOTS
    ends = []
    for box in range(BOXES):

        def enter(pair, end):
            numbers = [pairs[box, 0, pair], pairs[box, 1, pair]]
            for side in range(2):
                away = targets[box, side, pair] - here
                away = jnp.where(away >= all_slots // 2, away - all_slots, away)
                away = jnp.where(away < -(all_slots // 2), away + all_slots, away)
                hops = jnp.int32(-2)
                for low in range(-1, 3):
                    hops = hops + (away >= low * SLOTS).astype(jnp.int32)
                slot = away - hops * SLOTS
                hops = jnp.where(odd, hops, -hops)
                place = jnp.int32(len(places) * SLOTS)
                for n, want in enumerate(places):
                    place = jnp.where(hops == want, slot + n * SLOTS, place)
                entry = place * 128 + numbers[side] * 16 + numbers[1 - side] * 2
                if first_touch:
                    entry = entry + used[place]
                    used[place] = 1
                todo[box, end] = entry
                end = end + (place < len(places) * SLOTS).astype(jnp.int32)
            return end

        ends.append(lax.fori_loop(0, PAIRS, enter, jnp.int32(0), unroll=2))
    return ends


def listed(entry):
    return lax.shift_right_logical(entry, 7), lax.shift_right_logical(entry, 4) & 7, lax.shift_right_logical(entry, 1) & 7


def front_kernel(targets_h, pairs_h, split_h, interp_h, cols_h, rows_h, inverse_h,
                 near_out, over_out, far_out, edge_out, partner_out,
                 interp, cols, rows, inverse, w_far, y_near, compressor, grams, split, acc, targets, pairs, todo, used,
                 near_head, far_head, edge_head, partner_head, in_sems, out_sems, small_sems):
    small = [
        pltpu.make_async_copy(targets_h, targets, small_sems.at[0]),
        pltpu.make_async_copy(pairs_h, pairs, small_sems.at[1]),
        pltpu.make_async_copy(split_h, split, small_sems.at[2]),
    ]
    for copy in small:
        copy.start()
    copies = input_copies((interp_h, cols_h, rows_h, inverse_h), (interp, cols, rows, inverse), in_sems)
    for box in range(BOXES):
        for copy in copies[box]:
            copy.start()

    def clear_used(n, _):
        used[n] = 0
        return 0

    lax.fori_loop(0, 4 * SLOTS, clear_used, 0, unroll=8)
    for copy in small:
        copy.wait()
    ends = work_list(targets, pairs, todo, used, (2, -2, 1, -1), True)

    def number(n, counts):
        name = n.astype(F32)
        near_head[0, counts[0]] = name
        edge_head[1, counts[0]] = name
        far_head[0, counts[1]] = name
        edge_head[0, counts[2]] = name
        partner_head[0, counts[3]] = name
        return tuple(count + used[base * SLOTS + n] for base, count in enumerate(counts))

    counts = lax.fori_loop(0, SLOTS, number, (jnp.int32(0),) * 4, unroll=4)
    rows_of = (near_head.at[0], far_head.at[0], edge_head.at[0], partner_head.at[0], edge_head.at[1])
    for row, count in zip(rows_of, (*counts, counts[0])):

        def blank(n, _):
            row[n] = -1.0
            return 0

        lax.fori_loop(count, CAP, blank, 0)

    far_head[1, 0] = counts[1].astype(F32)
    edge_head[2, 0] = counts[2].astype(F32)
    edge_head[2, 1] = jnp.maximum(counts[0] - NEAR, 0).astype(F32)
    for box in range(BOXES):
        products(box, copies[box], split, interp, inverse, rows, cols, w_far, y_near, compressor, grams)

        def add(n, _):
            entry = todo[box, n]
            place, i, j = listed(entry)
            acc[place] = jnp.where((entry & 1) == 1, acc[place], 0.0) - grams[i, j]
            return 0

        lax.fori_loop(0, ends[box], add, 0)

    labels = [
        pltpu.make_async_copy(near_head, near_out.at[pl.ds(0, HEAD)], small_sems.at[0]),
        pltpu.make_async_copy(far_head, far_out.at[pl.ds(0, HEAD)], small_sems.at[1]),
        pltpu.make_async_copy(edge_head, edge_out.at[pl.ds(0, HEAD)], small_sems.at[2]),
        pltpu.make_async_copy(partner_head, partner_out.at[pl.ds(0, HEAD)], small_sems.at[3]),
    ]
    for copy in labels:
        copy.start()
    near_count = jnp.minimum(counts[0], NEAR)
    lots = (
        (0, near_head, near_out, 0, near_count),
        (0, near_head, over_out, NEAR, counts[0]),
        (1, far_head, far_out, 0, counts[1]),
        (2, edge_head, edge_out, 0, counts[2]),
        (3, partner_head, partner_out, 0, counts[3]),
    )
    for base, head, out, begin, end in lots:

        def send(n, _):
            source = acc.at[base * SLOTS + head[0, n].astype(jnp.int32)]
            rows_at = block(n - begin) if begin else payload_block(n)
            pltpu.make_async_copy(source, out.at[rows_at], out_sems.at[base, n]).start()
            return 0

        lax.fori_loop(begin, end, send, 0)
    for base in range(4):

        def drain(n, _):
            pltpu.make_async_copy(acc.at[base], far_out.at[payload_block(0)], out_sems.at[base, n]).wait()
            return 0

        lax.fori_loop(0, counts[base], drain, 0)
    for copy in labels:
        copy.wait()


def box_scratch():
    return [
        pltpu.VMEM((BOXES, RD, SK), BF16),
        pltpu.VMEM((BOXES, ROWS, P_SIZE), BF16),
        pltpu.VMEM((BOXES, ROWS, P_SIZE), BF16),
        pltpu.VMEM((BOXES, RD, RD), BF16),
        pltpu.VMEM((ROWS, RD), BF16),
        pltpu.VMEM((ROWS, RD), BF16),
        pltpu.VMEM((P_SIZE, RD), BF16),
        pltpu.VMEM((NB, NB, SK, SK), F32),
    ]


def front(targets, pairs, split, interp, cols, rows, inverse):
    return pl.pallas_call(
        front_kernel,
        out_shape=(
            payload_type(NEAR), jax.ShapeDtypeStruct((OVER * SK, SK), F32),
            payload_type(CAP), payload_type(CAP), payload_type(CAP),
        ),
        in_specs=[ANY] * 7,
        out_specs=(ANY,) * 5,
        scratch_shapes=box_scratch() + [
            pltpu.VMEM((BOXES, P_SIZE), jnp.int32),
            pltpu.VMEM((4 * SLOTS + 1, SK, SK), F32),
            pltpu.SMEM((BOXES, 2, PAIRS), jnp.int32),
            pltpu.SMEM((BOXES, 2, PAIRS), jnp.int32),
            pltpu.SMEM((BOXES, 2 * PAIRS + 1), jnp.int32),
            pltpu.SMEM((4 * SLOTS + 1,), jnp.int32),
            pltpu.SMEM((HEAD, 128), F32),
            pltpu.SMEM((HEAD, 128), F32),
            pltpu.SMEM((HEAD, 128), F32),
            pltpu.SMEM((HEAD, 128), F32),
            pltpu.SemaphoreType.DMA((BOXES, 4)),
            pltpu.SemaphoreType.DMA((4, CAP)),
            pltpu.SemaphoreType.DMA((4,)),
        ],
        compiler_params=pltpu.CompilerParams(vmem_limit_bytes=VMEM_BYTES),
        cost_estimate=cost(1),
        name="front",
    )(targets, pairs, split, interp, cols, rows, inverse)


def rest_kernel(targets_h, pairs_h, split_h, interp_h, cols_h, rows_h, inverse_h, self_h, start_h,
                total_out, coarse_out, skel_out,
                interp, cols, rows, inverse, self_block, w_far, y_near, compressor, grams, split, start, acc, skel,
                targets, pairs, todo, in_sems, out_sems, small_sems):
    small = [
        pltpu.make_async_copy(targets_h, targets, small_sems.at[0]),
        pltpu.make_async_copy(pairs_h, pairs, small_sems.at[1]),
        pltpu.make_async_copy(split_h, split, small_sems.at[2]),
    ]
    for copy in small:
        copy.start()
    copies = input_copies((interp_h, cols_h, rows_h, inverse_h, self_h), (interp, cols, rows, inverse, self_block), in_sems)
    start_copy = pltpu.make_async_copy(start_h, start, out_sems.at[4])
    for copy in copies[0]:
        copy.start()
    start_copy.start()
    for copy in copies[1]:
        copy.start()

    for copy in small:
        copy.wait()
    ends = work_list(targets, pairs, todo, None, (0,), False)
    start_copy.wait()

    def widen(n, _):
        acc[n] = start[n].astype(F32)
        return 0

    lax.fori_loop(0, SLOTS, widen, 0)
    parity = lax.rem(lax.axis_index("box"), 2)
    for box in range(BOXES):
        pick_skel = products(box, copies[box], split, interp, inverse, rows, cols, w_far, y_near, compressor, grams)

        def add(n, _):
            place, i, j = listed(todo[box, n])
            acc[place] = acc[place] - grams[i, j]
            return 0

        lax.fori_loop(0, ends[box], add, 0)
        copies[box][4].wait()
        x_self = mul(self_block[box], compressor[...]).astype(BF16)
        y_self = mul(x_self, inverse[box]).astype(BF16)
        pick_rows = pick_skel.astype(F32).T.astype(BF16)
        for n in range(ROWS // TILE):
            at = slice(n * TILE, (n + 1) * TILE)
            base = lax.dot_general(pick_rows, cols[box, at, :], NT, preferred_element_type=F32)
            base = base - lax.dot_general(y_self, w_far[at, :], NT, preferred_element_type=F32)
            for k in range(TILE // SK):
                j = n * (TILE // SK) + k
                skel[j // 4, box, j % 4] = base[:, k * SK:(k + 1) * SK]

    outs = [
        pltpu.make_async_copy(acc, total_out, out_sems.at[1]),
        pltpu.make_async_copy(skel.at[parity], coarse_out.at[pl.ds(2 * parity, 2)], out_sems.at[2]),
        pltpu.make_async_copy(skel.at[1 - parity], skel_out, out_sems.at[3]),
    ]
    for copy in outs:
        copy.start()
    for copy in outs:
        copy.wait()


def rest(targets, pairs, split, interp, cols, rows, inverse, self_block, start):
    scratch = box_scratch()
    scratch.insert(4, pltpu.VMEM((BOXES, SK, P_SIZE), BF16))
    return pl.pallas_call(
        rest_kernel,
        out_shape=(
            block_type(SLOTS),
            jax.ShapeDtypeStruct((2 * BOXES, NB // 2, SK, SK), F32),
            jax.ShapeDtypeStruct((BOXES, NB // 2, SK, SK), F32),
        ),
        in_specs=[ANY] * 9,
        out_specs=(ANY,) * 3,
        scratch_shapes=scratch + [
            pltpu.VMEM((BOXES, P_SIZE), jnp.int32),
            pltpu.VMEM((SLOTS, SK, SK), BF16),
            pltpu.VMEM((SLOTS, SK, SK), F32),
            pltpu.VMEM((2, BOXES, NB // 2, SK, SK), F32),
            pltpu.SMEM((BOXES, 2, PAIRS), jnp.int32),
            pltpu.SMEM((BOXES, 2, PAIRS), jnp.int32),
            pltpu.SMEM((BOXES, 2 * PAIRS + 1), jnp.int32),
            pltpu.SemaphoreType.DMA((BOXES, 5)),
            pltpu.SemaphoreType.DMA((5,)),
            pltpu.SemaphoreType.DMA((3,)),
        ],
        compiler_params=pltpu.CompilerParams(vmem_limit_bytes=VMEM_BYTES),
        cost_estimate=cost(1),
        name="rest",
    )(targets, pairs, split, interp, cols, rows, inverse, self_block, start)


def merge_kernel(over_h, edge_h, far_h, first_out, second_out, *refs):
    tail_outs = refs[:len(TAILS)]
    tail_count, blocks, edge_head, far_head, head, places, sources, in_sems, out_sems, tail_sems = refs[len(TAILS):]
    heads = [
        pltpu.make_async_copy(edge_h.at[pl.ds(0, HEAD)], edge_head, in_sems.at[0]),
        pltpu.make_async_copy(far_h.at[pl.ds(0, HEAD)], far_head, in_sems.at[1]),
    ]
    bulk = [
        pltpu.make_async_copy(over_h, blocks.at[pl.ds(0, OVER * SK)], in_sems.at[2]),
        pltpu.make_async_copy(edge_h.at[pl.ds(HEAD, CAP * SK)], blocks.at[pl.ds(OVER * SK, CAP * SK)], in_sems.at[3]),
        pltpu.make_async_copy(far_h.at[pl.ds(HEAD, CAP * SK)], blocks.at[pl.ds((OVER + CAP) * SK, CAP * SK)], in_sems.at[4]),
    ]
    for copy in heads + bulk:
        copy.start()

    def clear(n, _):
        places[n] = -1
        return 0

    lax.fori_loop(0, SLOTS, clear, 0, unroll=8)
    for copy in heads:
        copy.wait()

    over_count = edge_head[2, 1].astype(jnp.int32)
    edge_count = edge_head[2, 0].astype(jnp.int32)

    def take_over(n, _):
        head[0, n] = edge_head[1, NEAR + n] + MARK
        sources[n] = n
        return 0

    lax.fori_loop(0, over_count, take_over, 0)

    def take_edge(n, _):
        slot = edge_head[0, n]
        head[0, over_count + n] = slot
        sources[over_count + n] = OVER + n
        places[slot.astype(jnp.int32)] = OVER + n
        return 0

    lax.fori_loop(0, edge_count, take_edge, 0)
    for copy in bulk:
        copy.wait()

    def take_far(n, count):
        slot = far_head[0, n]
        place = places[slot.astype(jnp.int32)]
        head[0, count] = slot
        sources[count] = OVER + CAP + n

        @pl.when(place >= 0)
        def _():
            blocks[block(place), :] = blocks[block(place), :] + blocks[block(OVER + CAP + n), :]

        return count + (place < 0).astype(jnp.int32)

    count = lax.fori_loop(0, far_head[1, 0].astype(jnp.int32), take_far, over_count + edge_count)

    def blank(n, _):
        head[0, n] = -1.0
        return 0

    lax.fori_loop(count, SLOTS + OVER, blank, 0)
    left = jnp.maximum(count - FIXED, 0)
    tail_count[0] = left
    head[1, 0] = left.astype(F32)
    label = pltpu.make_async_copy(head, first_out.at[pl.ds(0, HEAD)], in_sems.at[0])
    label.start()

    def send_first(n, _):
        pltpu.make_async_copy(blocks.at[block(sources[n])], first_out.at[payload_block(n)], out_sems.at[n]).start()
        return 0

    def send_second(n, _):
        pltpu.make_async_copy(blocks.at[block(sources[n])], second_out.at[block(n - PART)], out_sems.at[n]).start()
        return 0

    lax.fori_loop(0, jnp.minimum(count, PART), send_first, 0)
    lax.fori_loop(PART, jnp.minimum(count, FIXED), send_second, 0)

    def send_tail(n, _):
        for k, (size, out) in enumerate(zip(TAILS, tail_outs)):

            @pl.when(left <= size)
            def _():
                source = blocks.at[block(sources[FIXED + n])]
                pltpu.make_async_copy(source, out.at[block(n)], tail_sems.at[k, n]).start()

        return 0

    lax.fori_loop(0, left, send_tail, 0)

    def drain(n, _):
        pltpu.make_async_copy(blocks.at[block(0)], second_out.at[block(0)], out_sems.at[n]).wait()
        return 0

    lax.fori_loop(0, jnp.minimum(count, FIXED), drain, 0)

    def drain_tail(n, _):
        for k, size in enumerate(TAILS):

            @pl.when(left <= size)
            def _():
                pltpu.make_async_copy(blocks.at[block(0)], second_out.at[block(0)], tail_sems.at[k, n]).wait()

        return 0

    lax.fori_loop(0, left, drain_tail, 0)
    label.wait()


def merge(over, edge, far):
    return pl.pallas_call(
        merge_kernel,
        out_shape=(
            payload_type(PART),
            jax.ShapeDtypeStruct((SECOND * SK, SK), F32),
            *[jax.ShapeDtypeStruct((size * SK, SK), F32) for size in TAILS],
            jax.ShapeDtypeStruct((1,), jnp.int32),
        ),
        in_specs=[ANY] * 3,
        out_specs=(ANY,) * (2 + len(TAILS)) + (SMEM,),
        scratch_shapes=[
            pltpu.VMEM(((OVER + 2 * CAP) * SK, SK), F32),
            pltpu.SMEM((HEAD, 128), F32),
            pltpu.SMEM((HEAD, 128), F32),
            pltpu.SMEM((HEAD, 128), F32),
            pltpu.SMEM((SLOTS,), jnp.int32),
            pltpu.SMEM((SLOTS + OVER + 1,), jnp.int32),
            pltpu.SemaphoreType.DMA((5,)),
            pltpu.SemaphoreType.DMA((FIXED,)),
            pltpu.SemaphoreType.DMA((len(TAILS), TAILS[-1])),
        ],
        compiler_params=pltpu.CompilerParams(vmem_limit_bytes=VMEM_BYTES),
        cost_estimate=cost(1),
        name="merge",
    )(over, edge, far)


def settle_kernel(total_h, *refs):
    count = len(PARCELS)
    payloads, out, total = refs[:count], refs[count], refs[count + 1]
    blocks, heads, sems = refs[count + 2:2 * count + 2], refs[2 * count + 2:3 * count + 2], refs[-1]
    loads = [pltpu.make_async_copy(total_h, total, sems.at[0])]
    for n in range(count):
        loads.append(pltpu.make_async_copy(payloads[n].at[pl.ds(0, HEAD)], heads[n], sems.at[2 * n + 1]))
        size = PARCELS[n][0] * SK
        loads.append(pltpu.make_async_copy(payloads[n].at[pl.ds(HEAD, size)], blocks[n], sems.at[2 * n + 2]))
    for copy in loads:
        copy.start()
    loads[0].wait()
    for n, (size, base) in enumerate(PARCELS):
        loads[2 * n + 1].wait()
        loads[2 * n + 2].wait()

        def add(k, _):
            slot = heads[n][0, k].astype(jnp.int32) - base

            @pl.when((slot >= 0) & (slot < SLOTS))
            def _():
                total[slot] = total[slot] + blocks[n][block(k), :]

            return 0

        lax.fori_loop(0, size, add, 0)
    copy = pltpu.make_async_copy(total, out, sems.at[0])
    copy.start()
    copy.wait()


def settle(total, *payloads):
    return pl.pallas_call(
        settle_kernel,
        out_shape=block_type(SLOTS),
        in_specs=[ANY] * (1 + len(PARCELS)),
        out_specs=ANY,
        scratch_shapes=[
            pltpu.VMEM((SLOTS, SK, SK), F32),
            *[pltpu.VMEM((size * SK, SK), F32) for size, _ in PARCELS],
            *[pltpu.SMEM((HEAD, 128), F32) for _ in PARCELS],
            pltpu.SemaphoreType.DMA((1 + 2 * len(PARCELS),)),
        ],
        input_output_aliases={0: 0},
        compiler_params=pltpu.CompilerParams(vmem_limit_bytes=VMEM_BYTES),
        cost_estimate=cost(1),
        name="settle",
    )(total, *payloads)


def decide_kernel(own_count, first_h, near_h, total_h, forward_out, branch, held, head, sems):
    names = pltpu.make_async_copy(first_h.at[pl.ds(0, HEAD)], head, sems.at[0])
    part = pltpu.make_async_copy(first_h.at[pl.ds(0, HEAD + OVER * SK)], held, sems.at[1])
    names.start()
    part.start()
    names.wait()
    left = jnp.maximum(own_count[0], head[1, 0].astype(jnp.int32))
    which = jnp.int32(0)
    for size in (0, *TAILS[:-1]):
        which = which + (left > size).astype(jnp.int32)
    branch[0] = which
    part.wait()
    copy = pltpu.make_async_copy(held, forward_out, sems.at[0])
    copy.start()
    copy.wait()


def decide(own_count, first, near, total):
    return pl.pallas_call(
        decide_kernel,
        out_shape=(payload_type(OVER), jax.ShapeDtypeStruct((1,), jnp.int32)),
        in_specs=[SMEM, ANY, ANY, ANY],
        out_specs=(ANY, SMEM),
        scratch_shapes=[
            pltpu.VMEM((HEAD + OVER * SK, SK), F32),
            pltpu.SMEM((HEAD, 128), F32),
            pltpu.SemaphoreType.DMA((2,)),
        ],
        compiler_params=pltpu.CompilerParams(vmem_limit_bytes=VMEM_BYTES),
        cost_estimate=cost(1),
        name="decide",
    )(own_count, first, near, total)


def finish_kernel(begin, total_h, first_h, blocks_h, coarse_h, received, out, coarse_out,
                  total, blocks, head, sems, slot_sems, held, held_sems):
    other = lax.rem(lax.axis_index("box") + 1, 2)
    arrive = pltpu.make_async_copy(received, held, held_sems.at[0])
    arrive.start()

    def hand_over():
        arrive.wait()
        pltpu.make_async_copy(held, coarse_out.at[pl.ds(2 * other, 2)], held_sems.at[1]).start()

    add_late_kernel(begin, total_h, first_h, blocks_h, out, total, blocks, head, sems, slot_sems, hand_over)
    pltpu.make_async_copy(held, coarse_out.at[pl.ds(2 * other, 2)], held_sems.at[1]).wait()


def add_late_kernel(begin, total_h, first_h, blocks_h, out, total, blocks, head, sems, slot_sems, meanwhile=None):
    count = total.shape[0]
    names = pltpu.make_async_copy(first_h.at[pl.ds(0, HEAD)], head, sems.at[0])
    bulk = pltpu.make_async_copy(blocks_h, blocks, sems.at[1])
    names.start()
    bulk.start()
    names.wait()

    def each(act):
        def step(n, _):
            slot = head[0, begin + n].astype(jnp.int32)

            @pl.when((slot >= 0) & (slot < SLOTS))
            def _():
                act(n, slot)

            return 0

        lax.fori_loop(0, count, step, 0)

    def load(n, slot):
        pltpu.make_async_copy(total_h.at[slot], total.at[n], slot_sems.at[0, n]).start()

    def add(n, slot):
        pltpu.make_async_copy(total_h.at[slot], total.at[n], slot_sems.at[0, n]).wait()
        total[n] = total[n] + blocks[block(n), :]
        pltpu.make_async_copy(total.at[n], out.at[slot], slot_sems.at[1, n]).start()

    def drain(n, slot):
        pltpu.make_async_copy(total.at[n], out.at[slot], slot_sems.at[1, n]).wait()

    each(load)
    if meanwhile is not None:
        meanwhile()
    bulk.wait()
    each(add)
    each(drain)


def add_late(total, first, blocks, begin):
    count = blocks.shape[0] // SK
    return pl.pallas_call(
        functools.partial(add_late_kernel, begin),
        out_shape=block_type(SLOTS),
        in_specs=[ANY] * 3,
        out_specs=ANY,
        scratch_shapes=[
            pltpu.VMEM((count, SK, SK), F32),
            pltpu.VMEM((count * SK, SK), F32),
            pltpu.SMEM((HEAD, 128), F32),
            pltpu.SemaphoreType.DMA((2,)),
            pltpu.SemaphoreType.DMA((2, count)),
        ],
        input_output_aliases={0: 0},
        compiler_params=pltpu.CompilerParams(vmem_limit_bytes=VMEM_BYTES),
        cost_estimate=cost(1),
        name="add_late",
    )(total, first, blocks)


def finish(total, first, blocks, begin, coarse, received):
    count = blocks.shape[0] // SK
    return pl.pallas_call(
        functools.partial(finish_kernel, begin),
        out_shape=(block_type(SLOTS), jax.ShapeDtypeStruct(coarse.shape, F32)),
        in_specs=[ANY] * 5,
        out_specs=(ANY, ANY),
        scratch_shapes=[
            pltpu.VMEM((count, SK, SK), F32),
            pltpu.VMEM((count * SK, SK), F32),
            pltpu.SMEM((HEAD, 128), F32),
            pltpu.SemaphoreType.DMA((2,)),
            pltpu.SemaphoreType.DMA((2, count)),
            pltpu.VMEM(received.shape, F32),
            pltpu.SemaphoreType.DMA((2,)),
        ],
        input_output_aliases={0: 0, 3: 1},
        compiler_params=pltpu.CompilerParams(vmem_limit_bytes=VMEM_BYTES),
        cost_estimate=cost(1),
        name="finish",
    )(total, first, blocks, coarse, received)


def moved(value, route):
    devices = lax.axis_size("box")
    return lax.ppermute(value, "box", [(i, route(i) % devices) for i in range(devices)])


def other_core(i):
    return i ^ 1


def across(i):
    return i + 1 if i % 2 else i - 1


def beyond(i):
    return i + 2 if i % 2 else i - 2


def body(self_block, interp, split, inverse_block, row_blocks, col_blocks, pairs, targets, pair_blocks):
    targets = jnp.transpose(targets, (0, 2, 1))
    pairs = jnp.transpose(pairs, (0, 2, 1))
    rows = row_blocks.reshape(BOXES, ROWS, P_SIZE)
    cols = col_blocks.reshape(BOXES, ROWS, P_SIZE)
    near, over, far, edge, partner = front(targets, pairs, split, interp, cols, rows, inverse_block)
    near = moved(near, beyond)
    far = moved(far, other_core)
    partner = moved(partner, other_core)
    first, second, *tails, own_count = merge(over, edge, far)
    total, coarse, skel = rest(targets, pairs, split, interp, cols, rows, inverse_block, self_block, pair_blocks)
    first = moved(first, across)
    second = moved(second, across)
    skel = moved(skel, other_core)
    forward, branch = decide(own_count, first, near, total)
    forward = moved(forward, other_core)

    def none(total, near, partner, first, forward, *tails):
        return settle(total, near, partner, first, forward)

    def some(which):
        def send(total, near, partner, first, forward, *tails):
            tail = moved(tails[which], across)
            total = settle(total, near, partner, first, forward)
            return add_late(total, first, tail, FIXED)

        return send

    branches = [none] + [some(n) for n in range(len(TAILS))]
    total = lax.switch(branch[0], branches, total, near, partner, first, forward, *tails)
    total, coarse = finish(total, first, second, PART, coarse, skel)
    return total, coarse[None]


def solution(mesh):
    return jax.shard_map(
        body,
        mesh=mesh,
        in_specs=(
            P("box", None, None),
            P("box", None, None),
            P("box", None),
            P("box", None, None),
            P("box", None, None, None),
            P("box", None, None, None),
            P("box", None, None),
            P("box", None, None),
            P("box", None, None),
        ),
        out_specs=(P("box", None, None), P("box", None, None, None, None)),
        check_vma=False,
    )
```

```python
import functools

import jax
import jax.numpy as jnp
from jax import lax
from jax.experimental import pallas as pl
from jax.experimental.pallas import tpu as pltpu
from jax.sharding import PartitionSpec as P

P_SIZE = 512
SK = 128
RD = 384
BOXES = 2
NB = 8
PAIRS = 24
SLOTS = 48
CAP = 32
ROWS = NB * SK
TILE = 512
NEAR = 18
OVER = CAP - NEAR
PART = 14
SECOND = 18
FIXED = PART + SECOND
TAILS = (4, 7, 9, 10, 11, 12, 14, 17, 30)
MARK = 64
PARCELS = ((NEAR, 0), (CAP, 0), (PART, 0), (OVER, MARK))
HEAD = 8
VMEM_BYTES = 65_200_000
F32 = jnp.float32
BF16 = jnp.bfloat16
NT = (((1,), (1,)), ((), ()))

ANY = pl.BlockSpec(memory_space=pl.ANY)
SMEM = pl.BlockSpec(memory_space=pltpu.SMEM)


def block_type(count):
    return jax.ShapeDtypeStruct((count, SK, SK), F32)


def cost(us):
    return pl.CostEstimate(flops=us * 1_000_000_000, bytes_accessed=0, transcendentals=0)


def payload_type(count):
    return jax.ShapeDtypeStruct((HEAD + count * SK, SK), F32)


def input_copies(hbm, vmem, sems):
    out = []
    for box in range(BOXES):
        out.append([
            pltpu.make_async_copy(source.at[box], target.at[box], sems.at[box, n])
            for n, (source, target) in enumerate(zip(hbm, vmem))
        ])
    return out


def compressor_of(split, interp, box):
    points = lax.broadcasted_iota(jnp.int32, (P_SIZE, RD), 0)
    pick_red = points == split[box:box + 1, :RD]
    points = lax.broadcasted_iota(jnp.int32, (P_SIZE, SK), 0)
    pick_skel = (points == split[box:box + 1, RD:]).astype(F32).astype(BF16)
    spread = lax.dot_general(pick_skel, interp[box], NT, preferred_element_type=F32)
    return (jnp.where(pick_red, 1.0, 0.0) - spread).astype(BF16), pick_skel


def mul(a, b):
    return jnp.dot(a, b, preferred_element_type=F32)


def products(box, copies, split, interp, inverse, rows, cols, w_far, y_near, compressor, grams):
    copies[0].wait()
    comp, pick_skel = compressor_of(split, interp, box)
    compressor[...] = comp
    copies[1].wait()

    def far(n, _):
        at = pl.ds(pl.multiple_of(n * TILE, TILE), TILE)
        w_far[at, :] = mul(cols[box, at, :], compressor[...]).astype(BF16)
        return 0

    lax.fori_loop(0, ROWS // TILE, far, 0, unroll=True)
    copies[2].wait()
    copies[3].wait()

    def near(n, _):
        at = pl.ds(pl.multiple_of(n * TILE, TILE), TILE)
        x_near = mul(rows[box, at, :], compressor[...]).astype(BF16)
        y_near[at, :] = mul(x_near, inverse[box]).astype(BF16)
        return 0

    lax.fori_loop(0, ROWS // TILE, near, 0, unroll=True)

    def gram(n, _):
        at = pl.ds(pl.multiple_of(n * TILE, TILE), TILE)
        tile = lax.dot_general(y_near[...], w_far[at, :], NT, preferred_element_type=F32)
        for i in range(NB):
            for k in range(TILE // SK):
                grams[i, n * (TILE // SK) + k] = tile[i * SK:(i + 1) * SK, k * SK:(k + 1) * SK]
        return 0

    lax.fori_loop(0, ROWS // TILE, gram, 0, unroll=True)
    return pick_skel


def block(n):
    return pl.ds(pl.multiple_of(n * SK, SK), SK)


def payload_block(n):
    return pl.ds(pl.multiple_of(HEAD + n * SK, 8), SK)


def work_list(targets, pairs, todo, used, places, first_touch):
    device = lax.axis_index("box")
    odd = lax.rem(device, 2) == 1
    all_slots = lax.axis_size("box") * SLOTS
    here = device * SLOTS
    ends = []
    for box in range(BOXES):

        def enter(pair, end):
            numbers = [pairs[box, 0, pair], pairs[box, 1, pair]]
            for side in range(2):
                away = targets[box, side, pair] - here
                away = jnp.where(away >= all_slots // 2, away - all_slots, away)
                away = jnp.where(away < -(all_slots // 2), away + all_slots, away)
                hops = jnp.int32(-2)
                for low in range(-1, 3):
                    hops = hops + (away >= low * SLOTS).astype(jnp.int32)
                slot = away - hops * SLOTS
                hops = jnp.where(odd, hops, -hops)
                place = jnp.int32(len(places) * SLOTS)
                for n, want in enumerate(places):
                    place = jnp.where(hops == want, slot + n * SLOTS, place)
                entry = place * 128 + numbers[side] * 16 + numbers[1 - side] * 2
                if first_touch:
                    entry = entry + used[place]
                    used[place] = 1
                todo[box, end] = entry
                end = end + (place < len(places) * SLOTS).astype(jnp.int32)
            return end

        ends.append(lax.fori_loop(0, PAIRS, enter, jnp.int32(0), unroll=2))
    return ends


def listed(entry):
    return lax.shift_right_logical(entry, 7), lax.shift_right_logical(entry, 4) & 7, lax.shift_right_logical(entry, 1) & 7


def front_kernel(targets_h, pairs_h, split_h, interp_h, cols_h, rows_h, inverse_h,
                 near_out, over_out, far_out, edge_out, partner_out,
                 interp, cols, rows, inverse, w_far, y_near, compressor, grams, split, acc, targets, pairs, todo, used,
                 near_head, far_head, edge_head, partner_head, in_sems, out_sems, small_sems):
    small = [
        pltpu.make_async_copy(targets_h, targets, small_sems.at[0]),
        pltpu.make_async_copy(pairs_h, pairs, small_sems.at[1]),
        pltpu.make_async_copy(split_h, split, small_sems.at[2]),
    ]
    for copy in small:
        copy.start()
    copies = input_copies((interp_h, cols_h, rows_h, inverse_h), (interp, cols, rows, inverse), in_sems)
    for box in range(BOXES):
        for copy in copies[box]:
            copy.start()

    def clear_used(n, _):
        used[n] = 0
        return 0

    lax.fori_loop(0, 4 * SLOTS, clear_used, 0, unroll=8)
    for copy in small:
        copy.wait()
    ends = work_list(targets, pairs, todo, used, (2, -2, 1, -1), True)

    def number(n, counts):
        name = n.astype(F32)
        near_head[0, counts[0]] = name
        edge_head[1, counts[0]] = name
        far_head[0, counts[1]] = name
        edge_head[0, counts[2]] = name
        partner_head[0, counts[3]] = name
        return tuple(count + used[base * SLOTS + n] for base, count in enumerate(counts))

    counts = lax.fori_loop(0, SLOTS, number, (jnp.int32(0),) * 4, unroll=4)
    rows_of = (near_head.at[0], far_head.at[0], edge_head.at[0], partner_head.at[0], edge_head.at[1])
    for row, count in zip(rows_of, (*counts, counts[0])):

        def blank(n, _):
            row[n] = -1.0
            return 0

        lax.fori_loop(count, CAP, blank, 0)

    far_head[1, 0] = counts[1].astype(F32)
    edge_head[2, 0] = counts[2].astype(F32)
    edge_head[2, 1] = jnp.maximum(counts[0] - NEAR, 0).astype(F32)
    for box in range(BOXES):
        products(box, copies[box], split, interp, inverse, rows, cols, w_far, y_near, compressor, grams)

        def add(n, _):
            entry = todo[box, n]
            place, i, j = listed(entry)
            acc[place] = jnp.where((entry & 1) == 1, acc[place], 0.0) - grams[i, j]
            return 0

        lax.fori_loop(0, ends[box], add, 0)

    labels = [
        pltpu.make_async_copy(near_head, near_out.at[pl.ds(0, HEAD)], small_sems.at[0]),
        pltpu.make_async_copy(far_head, far_out.at[pl.ds(0, HEAD)], small_sems.at[1]),
        pltpu.make_async_copy(edge_head, edge_out.at[pl.ds(0, HEAD)], small_sems.at[2]),
        pltpu.make_async_copy(partner_head, partner_out.at[pl.ds(0, HEAD)], small_sems.at[3]),
    ]
    for copy in labels:
        copy.start()
    near_count = jnp.minimum(counts[0], NEAR)
    lots = (
        (0, near_head, near_out, 0, near_count),
        (0, near_head, over_out, NEAR, counts[0]),
        (1, far_head, far_out, 0, counts[1]),
        (2, edge_head, edge_out, 0, counts[2]),
        (3, partner_head, partner_out, 0, counts[3]),
    )
    for base, head, out, begin, end in lots:

        def send(n, _):
            source = acc.at[base * SLOTS + head[0, n].astype(jnp.int32)]
            rows_at = block(n - begin) if begin else payload_block(n)
            pltpu.make_async_copy(source, out.at[rows_at], out_sems.at[base, n]).start()
            return 0

        lax.fori_loop(begin, end, send, 0)
    for base in range(4):

        def drain(n, _):
            pltpu.make_async_copy(acc.at[base], far_out.at[payload_block(0)], out_sems.at[base, n]).wait()
            return 0

        lax.fori_loop(0, counts[base], drain, 0)
    for copy in labels:
        copy.wait()


def box_scratch():
    return [
        pltpu.VMEM((BOXES, RD, SK), BF16),
        pltpu.VMEM((BOXES, ROWS, P_SIZE), BF16),
        pltpu.VMEM((BOXES, ROWS, P_SIZE), BF16),
        pltpu.VMEM((BOXES, RD, RD), BF16),
        pltpu.VMEM((ROWS, RD), BF16),
        pltpu.VMEM((ROWS, RD), BF16),
        pltpu.VMEM((P_SIZE, RD), BF16),
        pltpu.VMEM((NB, NB, SK, SK), F32),
    ]


def front(targets, pairs, split, interp, cols, rows, inverse):
    return pl.pallas_call(
        front_kernel,
        out_shape=(
            payload_type(NEAR), jax.ShapeDtypeStruct((OVER * SK, SK), F32),
            payload_type(CAP), payload_type(CAP), payload_type(CAP),
        ),
        in_specs=[ANY] * 7,
        out_specs=(ANY,) * 5,
        scratch_shapes=box_scratch() + [
            pltpu.VMEM((BOXES, P_SIZE), jnp.int32),
            pltpu.VMEM((4 * SLOTS + 1, SK, SK), F32),
            pltpu.SMEM((BOXES, 2, PAIRS), jnp.int32),
            pltpu.SMEM((BOXES, 2, PAIRS), jnp.int32),
            pltpu.SMEM((BOXES, 2 * PAIRS + 1), jnp.int32),
            pltpu.SMEM((4 * SLOTS + 1,), jnp.int32),
            pltpu.SMEM((HEAD, 128), F32),
            pltpu.SMEM((HEAD, 128), F32),
            pltpu.SMEM((HEAD, 128), F32),
            pltpu.SMEM((HEAD, 128), F32),
            pltpu.SemaphoreType.DMA((BOXES, 4)),
            pltpu.SemaphoreType.DMA((4, CAP)),
            pltpu.SemaphoreType.DMA((4,)),
        ],
        compiler_params=pltpu.CompilerParams(vmem_limit_bytes=VMEM_BYTES),
        cost_estimate=cost(1),
        name="front",
    )(targets, pairs, split, interp, cols, rows, inverse)


def rest_kernel(targets_h, pairs_h, split_h, interp_h, cols_h, rows_h, inverse_h, self_h, start_h,
                total_out, coarse_out, skel_out,
                interp, cols, rows, inverse, self_block, w_far, y_near, compressor, grams, split, start, acc, skel,
                targets, pairs, todo, in_sems, out_sems, small_sems):
    small = [
        pltpu.make_async_copy(targets_h, targets, small_sems.at[0]),
        pltpu.make_async_copy(pairs_h, pairs, small_sems.at[1]),
        pltpu.make_async_copy(split_h, split, small_sems.at[2]),
    ]
    for copy in small:
        copy.start()
    copies = input_copies((interp_h, cols_h, rows_h, inverse_h, self_h), (interp, cols, rows, inverse, self_block), in_sems)
    start_copy = pltpu.make_async_copy(start_h, start, out_sems.at[4])
    for copy in copies[0]:
        copy.start()
    start_copy.start()
    for copy in copies[1]:
        copy.start()

    for copy in small:
        copy.wait()
    ends = work_list(targets, pairs, todo, None, (0,), False)
    start_copy.wait()

    def widen(n, _):
        acc[n] = start[n].astype(F32)
        return 0

    lax.fori_loop(0, SLOTS, widen, 0)
    parity = lax.rem(lax.axis_index("box"), 2)
    for box in range(BOXES):
        pick_skel = products(box, copies[box], split, interp, inverse, rows, cols, w_far, y_near, compressor, grams)

        def add(n, _):
            place, i, j = listed(todo[box, n])
            acc[place] = acc[place] - grams[i, j]
            return 0

        lax.fori_loop(0, ends[box], add, 0)
        copies[box][4].wait()
        x_self = mul(self_block[box], compressor[...]).astype(BF16)
        y_self = mul(x_self, inverse[box]).astype(BF16)
        pick_rows = pick_skel.astype(F32).T.astype(BF16)
        for n in range(ROWS // TILE):
            at = slice(n * TILE, (n + 1) * TILE)
            base = lax.dot_general(pick_rows, cols[box, at, :], NT, preferred_element_type=F32)
            base = base - lax.dot_general(y_self, w_far[at, :], NT, preferred_element_type=F32)
            for k in range(TILE // SK):
                j = n * (TILE // SK) + k
                skel[j // 4, box, j % 4] = base[:, k * SK:(k + 1) * SK]

    outs = [
        pltpu.make_async_copy(acc, total_out, out_sems.at[1]),
        pltpu.make_async_copy(skel.at[parity], coarse_out.at[pl.ds(2 * parity, 2)], out_sems.at[2]),
        pltpu.make_async_copy(skel.at[1 - parity], skel_out, out_sems.at[3]),
    ]
    for copy in outs:
        copy.start()
    for copy in outs:
        copy.wait()


def rest(targets, pairs, split, interp, cols, rows, inverse, self_block, start):
    scratch = box_scratch()
    scratch.insert(4, pltpu.VMEM((BOXES, SK, P_SIZE), BF16))
    return pl.pallas_call(
        rest_kernel,
        out_shape=(
            block_type(SLOTS),
            jax.ShapeDtypeStruct((2 * BOXES, NB // 2, SK, SK), F32),
            jax.ShapeDtypeStruct((BOXES, NB // 2, SK, SK), F32),
        ),
        in_specs=[ANY] * 9,
        out_specs=(ANY,) * 3,
        scratch_shapes=scratch + [
            pltpu.VMEM((BOXES, P_SIZE), jnp.int32),
            pltpu.VMEM((SLOTS, SK, SK), BF16),
            pltpu.VMEM((SLOTS, SK, SK), F32),
            pltpu.VMEM((2, BOXES, NB // 2, SK, SK), F32),
            pltpu.SMEM((BOXES, 2, PAIRS), jnp.int32),
            pltpu.SMEM((BOXES, 2, PAIRS), jnp.int32),
            pltpu.SMEM((BOXES, 2 * PAIRS + 1), jnp.int32),
            pltpu.SemaphoreType.DMA((BOXES, 5)),
            pltpu.SemaphoreType.DMA((5,)),
            pltpu.SemaphoreType.DMA((3,)),
        ],
        compiler_params=pltpu.CompilerParams(vmem_limit_bytes=VMEM_BYTES),
        cost_estimate=cost(1),
        name="rest",
    )(targets, pairs, split, interp, cols, rows, inverse, self_block, start)


def merge_kernel(over_h, edge_h, far_h, first_out, second_out, *refs):
    tail_outs = refs[:len(TAILS)]
    tail_count, blocks, edge_head, far_head, head, places, sources, in_sems, out_sems, tail_sems = refs[len(TAILS):]
    heads = [
        pltpu.make_async_copy(edge_h.at[pl.ds(0, HEAD)], edge_head, in_sems.at[0]),
        pltpu.make_async_copy(far_h.at[pl.ds(0, HEAD)], far_head, in_sems.at[1]),
    ]
    bulk = [
        pltpu.make_async_copy(over_h, blocks.at[pl.ds(0, OVER * SK)], in_sems.at[2]),
        pltpu.make_async_copy(edge_h.at[pl.ds(HEAD, CAP * SK)], blocks.at[pl.ds(OVER * SK, CAP * SK)], in_sems.at[3]),
        pltpu.make_async_copy(far_h.at[pl.ds(HEAD, CAP * SK)], blocks.at[pl.ds((OVER + CAP) * SK, CAP * SK)], in_sems.at[4]),
    ]
    for copy in heads + bulk:
        copy.start()

    def clear(n, _):
        places[n] = -1
        return 0

    lax.fori_loop(0, SLOTS, clear, 0, unroll=8)
    for copy in heads:
        copy.wait()

    over_count = edge_head[2, 1].astype(jnp.int32)
    edge_count = edge_head[2, 0].astype(jnp.int32)

    def take_over(n, _):
        head[0, n] = edge_head[1, NEAR + n] + MARK
        sources[n] = n
        return 0

    lax.fori_loop(0, over_count, take_over, 0)

    def take_edge(n, _):
        slot = edge_head[0, n]
        head[0, over_count + n] = slot
        sources[over_count + n] = OVER + n
        places[slot.astype(jnp.int32)] = OVER + n
        return 0

    lax.fori_loop(0, edge_count, take_edge, 0)
    for copy in bulk:
        copy.wait()

    def take_far(n, count):
        slot = far_head[0, n]
        place = places[slot.astype(jnp.int32)]
        head[0, count] = slot
        sources[count] = OVER + CAP + n

        @pl.when(place >= 0)
        def _():
            blocks[block(place), :] = blocks[block(place), :] + blocks[block(OVER + CAP + n), :]

        return count + (place < 0).astype(jnp.int32)

    count = lax.fori_loop(0, far_head[1, 0].astype(jnp.int32), take_far, over_count + edge_count)

    def blank(n, _):
        head[0, n] = -1.0
        return 0

    lax.fori_loop(count, SLOTS + OVER, blank, 0)
    left = jnp.maximum(count - FIXED, 0)
    tail_count[0] = left
    head[1, 0] = left.astype(F32)
    label = pltpu.make_async_copy(head, first_out.at[pl.ds(0, HEAD)], in_sems.at[0])
    label.start()

    def send_first(n, _):
        pltpu.make_async_copy(blocks.at[block(sources[n])], first_out.at[payload_block(n)], out_sems.at[n]).start()
        return 0

    def send_second(n, _):
        pltpu.make_async_copy(blocks.at[block(sources[n])], second_out.at[block(n - PART)], out_sems.at[n]).start()
        return 0

    lax.fori_loop(0, jnp.minimum(count, PART), send_first, 0)
    lax.fori_loop(PART, jnp.minimum(count, FIXED), send_second, 0)

    def send_tail(n, _):
        for k, (size, out) in enumerate(zip(TAILS, tail_outs)):

            @pl.when(left <= size)
            def _():
                source = blocks.at[block(sources[FIXED + n])]
                pltpu.make_async_copy(source, out.at[block(n)], tail_sems.at[k, n]).start()

        return 0

    lax.fori_loop(0, left, send_tail, 0)

    def drain(n, _):
        pltpu.make_async_copy(blocks.at[block(0)], second_out.at[block(0)], out_sems.at[n]).wait()
        return 0

    lax.fori_loop(0, jnp.minimum(count, FIXED), drain, 0)

    def drain_tail(n, _):
        for k, size in enumerate(TAILS):

            @pl.when(left <= size)
            def _():
                pltpu.make_async_copy(blocks.at[block(0)], second_out.at[block(0)], tail_sems.at[k, n]).wait()

        return 0

    lax.fori_loop(0, left, drain_tail, 0)
    label.wait()


def merge(over, edge, far):
    return pl.pallas_call(
        merge_kernel,
        out_shape=(
            payload_type(PART),
            jax.ShapeDtypeStruct((SECOND * SK, SK), F32),
            *[jax.ShapeDtypeStruct((size * SK, SK), F32) for size in TAILS],
            jax.ShapeDtypeStruct((1,), jnp.int32),
        ),
        in_specs=[ANY] * 3,
        out_specs=(ANY,) * (2 + len(TAILS)) + (SMEM,),
        scratch_shapes=[
            pltpu.VMEM(((OVER + 2 * CAP) * SK, SK), F32),
            pltpu.SMEM((HEAD, 128), F32),
            pltpu.SMEM((HEAD, 128), F32),
            pltpu.SMEM((HEAD, 128), F32),
            pltpu.SMEM((SLOTS,), jnp.int32),
            pltpu.SMEM((SLOTS + OVER + 1,), jnp.int32),
            pltpu.SemaphoreType.DMA((5,)),
            pltpu.SemaphoreType.DMA((FIXED,)),
            pltpu.SemaphoreType.DMA((len(TAILS), TAILS[-1])),
        ],
        compiler_params=pltpu.CompilerParams(vmem_limit_bytes=VMEM_BYTES),
        cost_estimate=cost(1),
        name="merge",
    )(over, edge, far)


def settle_kernel(total_h, *refs):
    count = len(PARCELS)
    payloads, out, total = refs[:count], refs[count], refs[count + 1]
    blocks, heads, sems = refs[count + 2:2 * count + 2], refs[2 * count + 2:3 * count + 2], refs[-1]
    loads = [pltpu.make_async_copy(total_h, total, sems.at[0])]
    for n in range(count):
        loads.append(pltpu.make_async_copy(payloads[n].at[pl.ds(0, HEAD)], heads[n], sems.at[2 * n + 1]))
        size = PARCELS[n][0] * SK
        loads.append(pltpu.make_async_copy(payloads[n].at[pl.ds(HEAD, size)], blocks[n], sems.at[2 * n + 2]))
    for copy in loads:
        copy.start()
    loads[0].wait()
    for n, (size, base) in enumerate(PARCELS):
        loads[2 * n + 1].wait()
        loads[2 * n + 2].wait()

        def add(k, _):
            slot = heads[n][0, k].astype(jnp.int32) - base

            @pl.when((slot >= 0) & (slot < SLOTS))
            def _():
                total[slot] = total[slot] + blocks[n][block(k), :]

            return 0

        lax.fori_loop(0, size, add, 0)
    copy = pltpu.make_async_copy(total, out, sems.at[0])
    copy.start()
    copy.wait()


def settle(total, *payloads):
    return pl.pallas_call(
        settle_kernel,
        out_shape=block_type(SLOTS),
        in_specs=[ANY] * (1 + len(PARCELS)),
        out_specs=ANY,
        scratch_shapes=[
            pltpu.VMEM((SLOTS, SK, SK), F32),
            *[pltpu.VMEM((size * SK, SK), F32) for size, _ in PARCELS],
            *[pltpu.SMEM((HEAD, 128), F32) for _ in PARCELS],
            pltpu.SemaphoreType.DMA((1 + 2 * len(PARCELS),)),
        ],
        input_output_aliases={0: 0},
        compiler_params=pltpu.CompilerParams(vmem_limit_bytes=VMEM_BYTES),
        cost_estimate=cost(1),
        name="settle",
    )(total, *payloads)


def decide_kernel(own_count, first_h, near_h, total_h, forward_out, branch, held, head, sems):
    names = pltpu.make_async_copy(first_h.at[pl.ds(0, HEAD)], head, sems.at[0])
    part = pltpu.make_async_copy(first_h.at[pl.ds(0, HEAD + OVER * SK)], held, sems.at[1])
    names.start()
    part.start()
    names.wait()
    left = jnp.maximum(own_count[0], head[1, 0].astype(jnp.int32))
    which = jnp.int32(0)
    for size in (0, *TAILS[:-1]):
        which = which + (left > size).astype(jnp.int32)
    branch[0] = which
    part.wait()
    copy = pltpu.make_async_copy(held, forward_out, sems.at[0])
    copy.start()
    copy.wait()


def decide(own_count, first, near, total):
    return pl.pallas_call(
        decide_kernel,
        out_shape=(payload_type(OVER), jax.ShapeDtypeStruct((1,), jnp.int32)),
        in_specs=[SMEM, ANY, ANY, ANY],
        out_specs=(ANY, SMEM),
        scratch_shapes=[
            pltpu.VMEM((HEAD + OVER * SK, SK), F32),
            pltpu.SMEM((HEAD, 128), F32),
            pltpu.SemaphoreType.DMA((2,)),
        ],
        compiler_params=pltpu.CompilerParams(vmem_limit_bytes=VMEM_BYTES),
        cost_estimate=cost(1),
        name="decide",
    )(own_count, first, near, total)


def finish_kernel(begin, total_h, first_h, blocks_h, coarse_h, received, out, coarse_out,
                  total, blocks, head, sems, slot_sems, held, held_sems):
    other = lax.rem(lax.axis_index("box") + 1, 2)
    arrive = pltpu.make_async_copy(received, held, held_sems.at[0])
    arrive.start()

    def hand_over():
        arrive.wait()
        pltpu.make_async_copy(held, coarse_out.at[pl.ds(2 * other, 2)], held_sems.at[1]).start()

    add_late_kernel(begin, total_h, first_h, blocks_h, out, total, blocks, head, sems, slot_sems, hand_over)
    pltpu.make_async_copy(held, coarse_out.at[pl.ds(2 * other, 2)], held_sems.at[1]).wait()


def add_late_kernel(begin, total_h, first_h, blocks_h, out, total, blocks, head, sems, slot_sems, meanwhile=None):
    count = total.shape[0]
    names = pltpu.make_async_copy(first_h.at[pl.ds(0, HEAD)], head, sems.at[0])
    bulk = pltpu.make_async_copy(blocks_h, blocks, sems.at[1])
    names.start()
    bulk.start()
    names.wait()

    def each(act):
        def step(n, _):
            slot = head[0, begin + n].astype(jnp.int32)

            @pl.when((slot >= 0) & (slot < SLOTS))
            def _():
                act(n, slot)

            return 0

        lax.fori_loop(0, count, step, 0)

    def load(n, slot):
        pltpu.make_async_copy(total_h.at[slot], total.at[n], slot_sems.at[0, n]).start()

    def add(n, slot):
        pltpu.make_async_copy(total_h.at[slot], total.at[n], slot_sems.at[0, n]).wait()
        total[n] = total[n] + blocks[block(n), :]
        pltpu.make_async_copy(total.at[n], out.at[slot], slot_sems.at[1, n]).start()

    def drain(n, slot):
        pltpu.make_async_copy(total.at[n], out.at[slot], slot_sems.at[1, n]).wait()

    each(load)
    if meanwhile is not None:
        meanwhile()
    bulk.wait()
    each(add)
    each(drain)


def add_late(total, first, blocks, begin):
    count = blocks.shape[0] // SK
    return pl.pallas_call(
        functools.partial(add_late_kernel, begin),
        out_shape=block_type(SLOTS),
        in_specs=[ANY] * 3,
        out_specs=ANY,
        scratch_shapes=[
            pltpu.VMEM((count, SK, SK), F32),
            pltpu.VMEM((count * SK, SK), F32),
            pltpu.SMEM((HEAD, 128), F32),
            pltpu.SemaphoreType.DMA((2,)),
            pltpu.SemaphoreType.DMA((2, count)),
        ],
        input_output_aliases={0: 0},
        compiler_params=pltpu.CompilerParams(vmem_limit_bytes=VMEM_BYTES),
        cost_estimate=cost(1),
        name="add_late",
    )(total, first, blocks)


def finish(total, first, blocks, begin, coarse, received):
    count = blocks.shape[0] // SK
    return pl.pallas_call(
        functools.partial(finish_kernel, begin),
        out_shape=(block_type(SLOTS), jax.ShapeDtypeStruct(coarse.shape, F32)),
        in_specs=[ANY] * 5,
        out_specs=(ANY, ANY),
        scratch_shapes=[
            pltpu.VMEM((count, SK, SK), F32),
            pltpu.VMEM((count * SK, SK), F32),
            pltpu.SMEM((HEAD, 128), F32),
            pltpu.SemaphoreType.DMA((2,)),
            pltpu.SemaphoreType.DMA((2, count)),
            pltpu.VMEM(received.shape, F32),
            pltpu.SemaphoreType.DMA((2,)),
        ],
        input_output_aliases={0: 0, 3: 1},
        compiler_params=pltpu.CompilerParams(vmem_limit_bytes=VMEM_BYTES),
        cost_estimate=cost(1),
        name="finish",
    )(total, first, blocks, coarse, received)


def moved(value, route):
    devices = lax.axis_size("box")
    return lax.ppermute(value, "box", [(i, route(i) % devices) for i in range(devices)])


def other_core(i):
    return i ^ 1


def across(i):
    return i + 1 if i % 2 else i - 1


def beyond(i):
    return i + 2 if i % 2 else i - 2


def body(self_block, interp, split, inverse_block, row_blocks, col_blocks, pairs, targets, pair_blocks):
    targets = jnp.transpose(targets, (0, 2, 1))
    pairs = jnp.transpose(pairs, (0, 2, 1))
    rows = row_blocks.reshape(BOXES, ROWS, P_SIZE)
    cols = col_blocks.reshape(BOXES, ROWS, P_SIZE)
    near, over, far, edge, partner = front(targets, pairs, split, interp, cols, rows, inverse_block)
    near = moved(near, beyond)
    far = moved(far, other_core)
    partner = moved(partner, other_core)
    first, second, *tails, own_count = merge(over, edge, far)
    total, coarse, skel = rest(targets, pairs, split, interp, cols, rows, inverse_block, self_block, pair_blocks)
    first = moved(first, across)
    second = moved(second, across)
    skel = moved(skel, other_core)
    forward, branch = decide(own_count, first, near, total)
    forward = moved(forward, other_core)

    def none(total, near, partner, first, forward, *tails):
        return settle(total, near, partner, first, forward)

    def some(which):
        def send(total, near, partner, first, forward, *tails):
            tail = moved(tails[which], across)
            total = settle(total, near, partner, first, forward)
            return add_late(total, first, tail, FIXED)

        return send

    branches = [none] + [some(n) for n in range(len(TAILS))]
    total = lax.switch(branch[0], branches, total, near, partner, first, forward, *tails)
    total, coarse = finish(total, first, second, PART, coarse, skel)
    return total, coarse[None]


def solution(mesh):
    return jax.shard_map(
        body,
        mesh=mesh,
        in_specs=(
            P("box", None, None),
            P("box", None, None),
            P("box", None),
            P("box", None, None),
            P("box", None, None, None),
            P("box", None, None, None),
            P("box", None, None),
            P("box", None, None),
            P("box", None, None),
        ),
        out_specs=(P("box", None, None), P("box", None, None, None, None)),
        check_vma=False,
    )
```
